128 devices in a mesh: gx: 2 (over core), gy: 2 (over x_hi), gz: 32 (over z, y, x_lo).
Axes of the slice: x: 4 (x_hi: 2, x_lo: 2; x = x_hi * 2 + x_lo), y: 4, z: 4, core: 2. Of those that a mesh axis runs over, the one named last changes fastest.
Arguments:
- charges: bfloat16 [32, 48, 8192], P('gx', 'gy', 'gz'), may hold values from -6 to 6
- kernel_fine: bfloat16 [9, 9, 9], replicated, may hold values from -0.21875 to 0.21875
- kernel_mid: bfloat16 [9, 9, 9], replicated, may hold values from -0.21875 to 0.21875
- gauss_width: float32 [8], replicated, may hold values from 1 to 256
- gauss_weight: float32 [8], replicated, may hold values from 0.25 to 2
Outputs:
- potential: float32 [32, 48, 8192], P('gx', 'gy', 'gz')
The draws below stay inside these ranges and needn't reach their ends.
All inputs are finite; a program needn't handle non-finite values.
Results may differ from the reference program's by a relative error of at most 0.002.
Values may be sent and summed in bfloat16 or wider, within the bound.
A program may use at most 384 MiB of HBM per device.

```python
import math
import jax
import jax.numpy as jnp
from jax import lax

M = 16
GAUSS = 8
NX = 32
NY = 48
NZ = 512
NX2 = 8
NY2 = 12
NZ2 = 128


def draw_gauss_width(key, part):
    offsets = jax.random.uniform(key, (GAUSS,), jnp.float32)
    levels = (jnp.arange(GAUSS, dtype=jnp.float32) + offsets) / GAUSS
    top = math.log(2.0 * NZ2)
    return jnp.clip(jnp.exp(levels * top), 1.0, 2.0 * NZ2).astype(jnp.float32)


def level_of(rng, shape, split, low, top_value):
    def one(axis_at, blocks):
        draws = jax.random.uniform(jax.random.fold_in(jax.random.fold_in(rng, 6), axis_at), (blocks,), jnp.float32, low / len(split), top_value / len(split))
        return jnp.repeat(jnp.exp(draws), shape[axis_at] // blocks).reshape((-1,) + (1,) * (len(shape) - axis_at - 1))

    gain = one(*split[0])
    for cut in split[1:]:
        gain = gain * one(*cut)
    return gain


def scatter_about(rng, dims, deviation, limit, pieces=(), kind=jnp.bfloat16):
    entries = deviation * jax.random.normal(rng, dims, jnp.float32)
    if pieces:
        entries = entries * level_of(rng, dims, pieces, -0.22, 0.18)
    return jnp.clip(entries, -limit, limit).astype(kind)


def setup_inputs(seed: int = 0) -> dict:
    splits = jax.random.split(jax.random.key(seed), 6)
    charges = scatter_about(splits[0], (NX, NY, NZ * M), 1.0, 6.0, ((0, 2), (1, 2), (2, 32)))
    kernel_fine = scatter_about(splits[1], (9, 9, 9), 729 ** -0.5, 0.21875)
    kernel_mid = scatter_about(splits[2], (9, 9, 9), 729 ** -0.5, 0.21875)
    gauss_width = draw_gauss_width(jax.random.fold_in(splits[5], 71), 0)
    gauss_weight = jnp.clip(jnp.exp(jax.random.uniform(splits[4], (GAUSS,), jnp.float32, math.log(0.25), math.log(2.0))), 0.25, 2.0)
    return {"charges": charges, "kernel_fine": kernel_fine, "kernel_mid": kernel_mid, "gauss_width": gauss_width, "gauss_weight": gauss_weight}


def stencil(offset):
    value = jnp.zeros(offset.shape, jnp.float32)
    value = jnp.where(jnp.abs(offset) == 1, 9.0 / 16.0, value)
    value = jnp.where(offset == 0, 1.0, value)
    value = jnp.where(jnp.abs(offset) == 3, -1.0 / 16.0, value)
    return value

def restriction(count):
    rows = jnp.arange(count // 2, dtype=jnp.int32)[:, None]
    cols = jnp.arange(count, dtype=jnp.int32)[None, :]
    return stencil(cols - 2 * rows)

def restrict_all(field):
    highest = lax.Precision.HIGHEST
    field = jnp.einsum('ia,abcm->ibcm', restriction(field.shape[0]), field, precision=highest)
    field = jnp.einsum('jb,ibcm->ijcm', restriction(field.shape[1]), field, precision=highest)
    field = jnp.einsum('kc,ijcm->ijkm', restriction(field.shape[2]), field, precision=highest)
    return field

def prolong_all(field):
    highest = lax.Precision.HIGHEST
    field = jnp.einsum('ai,abcm->ibcm', restriction(2 * field.shape[0]), field, precision=highest)
    field = jnp.einsum('bj,ibcm->ijcm', restriction(2 * field.shape[1]), field, precision=highest)
    field = jnp.einsum('ck,ijcm->ijkm', restriction(2 * field.shape[2]), field, precision=highest)
    return field

def correlate(field, kernel):
    source = jnp.transpose(field.astype(jnp.float32), (3, 0, 1, 2))[:, None]
    weights = kernel.astype(jnp.float32)[None, None]
    result = lax.conv_general_dilated(source, weights, (1, 1, 1), [(4, 4), (4, 4), (4, 4)], dimension_numbers=('NCDHW', 'OIDHW', 'NCDHW'), precision=lax.Precision.HIGHEST)
    return jnp.transpose(result[:, 0], (1, 2, 3, 0))

def gaussian(count, gauss_width):
    spots = jnp.arange(count, dtype=jnp.int32)
    spread = (spots[:, None] - spots[None, :]).astype(jnp.float32)
    width = gauss_width[:, None, None]
    return jnp.exp(-jnp.square(spread[None] / width)) / jnp.sqrt(width)

def reference(charges, kernel_fine, kernel_mid, gauss_width, gauss_weight):
    highest = lax.Precision.HIGHEST
    field = charges.reshape(NX, NY, NZ, M)
    short_fine = correlate(field, kernel_fine)
    q_mid = restrict_all(field.astype(jnp.float32)).astype(jnp.bfloat16)
    short_mid = correlate(q_mid, kernel_mid)
    q_top = restrict_all(q_mid.astype(jnp.float32))
    table_x = gaussian(NX2, gauss_width) * gauss_weight[:, None, None]
    section = jnp.einsum('gia,abcm->gibcm', table_x, q_top, precision=highest)
    section = jnp.einsum('gjb,gibcm->gijcm', gaussian(NY2, gauss_width), section, precision=highest)
    section = jnp.einsum('gkc,gijcm->gijkm', gaussian(NZ2, gauss_width), section, precision=highest)
    phi_top = lax.optimization_barrier(jnp.sum(section, axis=0))
    phi_mid = short_mid + prolong_all(phi_top)
    potential = short_fine + prolong_all(phi_mid)
    return potential.reshape(NX, NY, NZ * M)
```

```python
import jax
import jax.numpy as jnp
import numpy as np
import ml_dtypes
from jax import lax
from jax.experimental import pallas as pl
from jax.experimental.pallas import tpu as pltpu
from jax.sharding import PartitionSpec as P

M = 16
GAUSS = 8
MESH = pl.DeviceIdType.MESH
F32 = jnp.float32
BF16 = jnp.bfloat16


def weight(offset):
    return {0: 1.0, 1: 9 / 16, 3: -1 / 16}.get(abs(offset), 0.0)


def halo_list(side, size):
    if side == 0:
        return [size, size + 1, size + 2, size + 3, size + 5, None, None, None]
    return [-9, -7, -6, -5, -4, -3, -2, -1]


def extra_list(side, size):
    return [size + 1] if side == 0 else [-3, -1]


def cross(xs, ys):
    return [None if (x is None or y is None) else (x, y) for x in xs for y in ys]


def moved(coords, dx, dy):
    return [None if c is None else (c[0] + dx, c[1] + dy) for c in coords]


def padded(coords, size):
    return coords + [None] * (size - len(coords))


def picker(source, target):
    where = {c: i for i, c in enumerate(source) if c is not None}
    table = np.zeros((len(source), len(target)), np.float32)
    for j, c in enumerate(target):
        if c in where:
            table[where[c], j] = 1.0
    return table


def weights_between(fine, coarse):
    table = np.zeros((len(fine), len(coarse)), np.float32)
    for i, f in enumerate(fine):
        if f is None:
            continue
        for j, c in enumerate(coarse):
            if c is not None:
                table[i, j] = weight(f[0] - 2 * c[0]) * weight(f[1] - 2 * c[1])
    return table


ROWS_A = 512
ROWS_C = 2560


def plane(gx, gy):
    yl, xl = halo_list(gy, 24), halo_list(gx, 16)
    own = cross(range(16), range(24))
    fine = own + cross(range(16), yl) + cross(xl, list(range(24)) + yl)
    mid_own = cross(range(8), range(12))
    xs = list(range(8)) + extra_list(gx, 8)
    ys = list(range(12)) + extra_list(gy, 12)
    extra = [c for c in cross(xs, ys) if c not in set(mid_own)]
    mid = padded(mid_own, 128) + padded(extra, 128)
    return own, fine, mid_own, mid


def constants():
    whole = np.zeros((4, ROWS_C, 768), np.float32)
    spread = np.full((4, 32, 512), 1e30, np.float32)
    for gx in range(2):
        for gy in range(2):
            v = gx * 2 + gy
            own, fine, mid_own, mid = plane(gx, gy)
            out = whole[v]
            dy = 24 if gy == 0 else -24
            dx = 16 if gx == 0 else -16
            other_y = plane(gx, 1 - gy)[1]
            other_x = plane(1 - gx, gy)[1]
            out[0:384, 256:384] = picker(own, moved(other_y[384:512], 0, dy))
            out[0:512, 0:256] = picker(fine[:512], moved(other_x[512:768], dx, 0))
            xs = range(0, 7) if gx == 0 else range(-3, 4)
            ys = range(0, 9) if gy == 0 else range(-3, 6)
            window = padded(cross(xs, ys), 64)
            inside = cross(
                range(0, 10) if gx == 0 else range(-2, 8), range(0, 14) if gy == 0 else range(-2, 12)
            )
            up = weights_between(own, inside).astype(np.float64) @ weights_between(inside, window)
            up = np.concatenate([up, up], axis=1)
            high = up.astype(ml_dtypes.bfloat16).astype(np.float64)
            out[0:384, 384:512] = high
            out[0:384, 512:640] = up - high
            rz = np.zeros((256, 128), np.float32)
            for j in range(256):
                for i in range(128):
                    rz[j, i] = weight(j - 2 * i)
            out[0:256, 640:768] = rz
            out[512:1280, 0:256] = weights_between(fine, mid)
            top = padded(cross(range(4), range(6)), 32)
            out[512:768, 256:768] = np.tile(weights_between(mid, top), (1, 16))
            lanes = [c if c in set(inside) else None for c in cross(range(-2, 14), range(-2, 30))]
            out[768:1152, 256:768] = weights_between(own, lanes)
            out[1280:2048] = picker(fine, cross(range(-4, 20), range(-4, 28)))
            blocks = []
            for bx in (0, dx // 2):
                for by in (0, dy // 2):
                    blocks += padded(moved(mid_own, bx, by), 128)
            out[2048:2560] = picker(blocks, cross(range(-6, 18), range(-6, 26)))
            for i, c in enumerate(top):
                if c is None:
                    continue
                for wx in range(2):
                    for wy in range(2):
                        for xi in range(7):
                            for yi in range(9):
                                d = (4 * gx + c[0] - wx - xi) ** 2 + (6 * gy + c[1] - 3 * wy - yi) ** 2
                                lane = (wx * 2 + wy) * 128 + xi * 9 + yi
                                spread[v, i, lane] = d
                                spread[v, i, lane + 64] = d
    return whole.astype(ml_dtypes.bfloat16), spread


def dot(a, b):
    return lax.dot_general(a, b, (((1,), (0,)), ((), ())), preferred_element_type=F32)


def dot_t(a, b):
    return lax.dot_general(a, b, (((1,), (1,)), ((), ())), preferred_element_type=F32)


def split(a):
    high = a.astype(BF16)
    return high, (a - high.astype(F32)).astype(BF16)


def widen(a, count):
    near, far = 9.0 / 16.0, -1.0 / 16.0
    odd = near * (a[1 : count + 1] + a[2 : count + 2]) + far * (a[0:count] + a[3 : count + 3])
    return odd


def interleave(even, odd):
    both = jnp.concatenate([even[:, None], odd[:, None]], axis=1)
    return both.reshape((2 * even.shape[0],) + even.shape[1:])


def kernel(
    q_ref, kf_ref, km_ref, gw_ref, gg_ref, cst_hbm, spread_ref, out_ref,
    cst, fq, py, px, fpad, tfine, tmid, fm, mpad, gath, sfine, smid, amat, dmat, rmat, ezr, wlo, whi,
    cst_sem, s1, r1, s2, r2, sg, rg, s3, r3,
):
    gx, gy, gz = lax.axis_index("gx"), lax.axis_index("gy"), lax.axis_index("gz")
    nz = lax.axis_size("gz")
    ox, oy = 1 - gx, 1 - gy
    up, down = lax.rem(gz + 1, nz), lax.rem(gz + nz - 1, nz)
    variant = gx * 2 + gy

    barrier = pltpu.get_barrier_semaphore()
    for peer in ((ox, gy, gz), (gx, oy, gz), (ox, oy, gz), (gx, oy, up), (gx, oy, down)):
        pl.semaphore_signal(barrier, inc=1, device_id=peer, device_id_type=MESH)

    @pl.loop(1, nz)
    def _(d):
        pl.semaphore_signal(
            barrier, inc=1, device_id=(gx, gy, lax.rem(gz + d, nz)), device_id_type=MESH
        )

    first = pltpu.make_async_copy(
        cst_hbm.at[variant, pl.ds(0, ROWS_A)], cst.at[pl.ds(0, ROWS_A)], cst_sem.at[0]
    )
    rest = pltpu.make_async_copy(
        cst_hbm.at[variant, pl.ds(ROWS_A, ROWS_C - ROWS_A)],
        cst.at[pl.ds(ROWS_A, ROWS_C - ROWS_A)],
        cst_sem.at[1],
    )
    first.start()
    rest.start()

    turned = q_ref[...].astype(F32).reshape(384, 256).T.astype(BF16)
    fq[4:20, :, 0:384] = turned.reshape(16, 16, 384)
    first.wait()
    py[...] = dot(turned, cst[0:384, 256:384]).astype(BF16).reshape(16, 16, 128)

    def build(k_ref, table):
        lane = lax.broadcasted_iota(jnp.int32, (9, 512), 1)
        row = lax.broadcasted_iota(jnp.int32, (9, 512), 0)
        base = jnp.zeros((9, 512), F32)
        for a in range(9):
            place = (lane == row + 32 * a).astype(F32).astype(BF16)
            base = base + lax.dot_general(
                k_ref[a], place, (((0,), (0,)), ((), ())), preferred_element_type=F32
            )
        for c in range(9):
            strip = pltpu.roll(
                jnp.broadcast_to(base[c : c + 1], (8, 512)), 0, 1, stride=1, stride_axis=0
            )

            @pl.loop(0, 16)
            def _(i):
                low = pltpu.roll(strip, 16 * i, 1)
                high = pltpu.roll(strip, 16 * i + 8, 1)
                table[c, pl.ds(pl.multiple_of(16 * i, 16), 16), :] = jnp.concatenate(
                    [low, high], axis=0
                ).astype(BF16)

    build(kf_ref, tfine)

    pl.semaphore_wait(barrier, nz - 1 + 5)

    def send(src, dst, sems, recvs, i, peer):
        copy = pltpu.make_async_remote_copy(
            src_ref=src, dst_ref=dst, send_sem=sems.at[i], recv_sem=recvs.at[i],
            device_id=peer, device_id_type=MESH,
        )
        copy.start()
        return copy

    ways = [
        (py.at[12:16], fq.at[0:4, :, 384:512], (gx, oy, up)),
        (py.at[0:4], fq.at[20:24, :, 384:512], (gx, oy, down)),
        (fq.at[16:20, :, 0:384], fq.at[0:4, :, 0:384], (gx, gy, up)),
        (fq.at[4:8, :, 0:384], fq.at[20:24, :, 0:384], (gx, gy, down)),
        (py, fq.at[4:20, :, 384:512], (gx, oy, gz)),
    ]
    one = [send(src, dst, s1, r1, i, peer) for i, (src, dst, peer) in enumerate(ways)]

    build(km_ref, tmid)
    rest.wait()
    node = gz * 4 - 3 + lax.broadcasted_iota(jnp.int32, (16, 128), 0)
    gap = (node - lax.broadcasted_iota(jnp.int32, (16, 128), 1)).astype(F32)
    exists = (node >= 0) & (node < 4 * nz)
    half = lax.rem(lax.broadcasted_iota(jnp.int32, (32, 512), 1), 128) < 64
    parts = []
    for g in range(GAUSS):
        width = jnp.full((16, 128), gw_ref[g], F32)
        ratio = gap / width
        parts.append(jnp.where(exists, jnp.exp(-(ratio * ratio)) / jnp.sqrt(width), 0.0))
        width = jnp.full((32, 512), gw_ref[g], F32)
        both = jnp.exp(-(spread_ref[variant] / (width * width))) * (gg_ref[g] / width)
        for table, keep in ((wlo, half), (whi, jnp.logical_not(half))):
            high, low = split(jnp.where(keep, both, 0.0))
            table[0, 32 * g : 32 * g + 32] = high
            table[1, 32 * g : 32 * g + 32] = low
    ez = jnp.concatenate(parts, axis=0)
    rz = cst[0:256, 640:768]
    high, low = split(ez)
    low2 = (ez - high.astype(F32) - low.astype(F32)).astype(BF16)
    high, low = split(dot_t(high, rz) + dot_t(low, rz) + dot_t(low2, rz))
    ezr[0] = high
    ezr[1] = low

    for copy in one:
        copy.wait_recv()
    keep_low = (gz > 0).astype(F32).astype(BF16)
    keep_high = (gz < nz - 1).astype(F32).astype(BF16)
    fq[0:4, :, 0:512] = fq[0:4, :, 0:512] * keep_low
    fq[20:24, :, 0:512] = fq[20:24, :, 0:512] * keep_high
    known = fq[:, :, 0:512].reshape(384, 512)
    px[...] = dot(known, cst[0:512, 0:256]).astype(BF16).reshape(24, 16, 256)
    cross_x = send(px, fq.at[:, :, 512:768], s1, r1, 5, (ox, gy, gz))
    plane_mid = dot(known, cst[512:1024, 0:256])
    cross_x.wait_recv()
    plane_mid = plane_mid + dot(fq[:, :, 512:768].reshape(384, 256), cst[1024:1280, 0:256])
    rows = plane_mid.reshape(12, 2, 16, 256)
    even, odd = rows[:, 0], rows[:, 1]
    q_mid = (
        even[2:10]
        + (9.0 / 16.0) * (odd[1:9] + odd[2:10])
        + (-1.0 / 16.0) * (odd[0:8] + odd[3:11])
    ).astype(BF16)
    fm[6:14, :, 0:128] = q_mid[:, :, 0:128]
    tops = dot(q_mid.reshape(128, 256), cst[512:768, 256:768]).reshape(8, 16, 512)
    member = lax.broadcasted_iota(jnp.int32, (16, 512), 0)
    group = lax.broadcasted_iota(jnp.int32, (16, 512), 1) // 32
    gath[gz] = jnp.sum(jnp.where((member == group)[None], tops, 0.0), axis=1)

    def gather(d, slot):
        return pltpu.make_async_remote_copy(
            src_ref=gath.at[slot], dst_ref=gath.at[slot], send_sem=sg.at[d], recv_sem=rg.at[slot],
            device_id=(gx, gy, lax.rem(gz + d, nz)), device_id_type=MESH,
        )

    @pl.loop(1, nz)
    def _(d):
        gather(d, gz).start()

    ways = [
        (fm.at[8:14, :, 0:128], fm.at[0:6, :, 128:256], (gx, oy, up)),
        (fm.at[6:12, :, 0:128], fm.at[14:20, :, 128:256], (gx, oy, down)),
        (fm.at[8:14, :, 0:128], fm.at[0:6, :, 0:128], (gx, gy, up)),
        (fm.at[6:12, :, 0:128], fm.at[14:20, :, 0:128], (gx, gy, down)),
        (fm.at[6:14, :, 0:128], fm.at[6:14, :, 128:256], (gx, oy, gz)),
    ]
    two = [send(src, dst, s2, r2, i, peer) for i, (src, dst, peer) in enumerate(ways)]

    fpad[...] = dot(fq[...].reshape(384, 768), cst[1280:2048, :]).astype(BF16)
    sfine[...] = jnp.zeros_like(sfine)

    @pl.loop(0, 9)
    def _(c):
        rows_c = pl.ds(pl.multiple_of(c * 16, 16), 256)
        for g in range(2):
            sfine[g] += dot_t(tfine[c], fpad[rows_c, 256 * g : 256 * g + 512])

    for copy in two:
        copy.wait_recv()
    fm[0:6, :, 0:256] = fm[0:6, :, 0:256] * keep_low
    fm[14:20, :, 0:256] = fm[14:20, :, 0:256] * keep_high
    cross_m = send(fm.at[:, :, 0:256], fm.at[:, :, 256:512], s2, r2, 5, (ox, gy, gz))

    @pl.loop(1, nz)
    def _(d):
        gather(d, lax.rem(gz + nz - d, nz)).wait_recv()

    high, low = split(gath[...].reshape(256, 512))
    fields = dot(ezr[0], high) + (dot(ezr[0], low) + dot(ezr[1], high))
    lane = lax.broadcasted_iota(jnp.int32, (16, 128), 1) // 32
    for j in range(4):
        tile = fields[:, 128 * j : 128 * j + 128]
        turns = [tile] + [pltpu.roll(tile, 32 * t, 1) for t in range(1, 4)]
        for i in range(4):
            m = 4 * j + i
            for t in range(2):
                block = None
                for s in range(4):
                    g = 4 * t + s
                    piece = turns[(s - i) % 4][16 * g : 16 * g + 16]
                    block = piece if block is None else jnp.where(lane == s, piece, block)
                amat[16 * m : 16 * m + 16, 128 * t : 128 * t + 128] = block
    high, low = split(amat[...])
    share = dot(high[0:128], wlo[0]) + dot(high[128:256], whi[0])
    share = share + (dot(low[0:128], wlo[0]) + dot(low[128:256], whi[0]))
    share = share + (dot(high[0:128], wlo[1]) + dot(high[128:256], whi[1]))
    share = jnp.swapaxes(share.reshape(8, 16, 512), 0, 1)
    for w in range(4):
        dmat[w] = share[0:10, :, 128 * w : 128 * w + 128]
    ways = [(oy + 2 * gx, (gx, oy, gz)), (oy + 2 * ox, (ox, oy, gz)), (gy + 2 * ox, (ox, gy, gz))]
    three = [send(dmat.at[w], rmat.at[i], s3, r3, i, peer) for i, (w, peer) in enumerate(ways)]

    cross_m.wait_recv()
    mpad[...] = dot(fm[...].reshape(320, 512), cst[2048:2560, :]).astype(BF16)
    smid[...] = jnp.zeros_like(smid)

    @pl.loop(0, 9)
    def _(c):
        rows_c = pl.ds(pl.multiple_of(c * 16, 16), 192)
        for g in range(2):
            smid[:, 256 * g : 256 * g + 256] += dot_t(
                mpad[rows_c, 256 * g : 256 * g + 512], tmid[c]
            )

    def trimmed(mid):
        spot = lax.broadcasted_iota(jnp.int32, mid.shape, 0) - 2 + 8 * gz
        return jnp.where((spot >= 0) & (spot < 8 * nz), mid, 0.0)

    mid = trimmed(smid[...].reshape(12, 16, 512))
    fine = interleave(mid[2:10], widen(mid[1:12], 8)).reshape(256, 512)
    high, low = split(fine)
    back = cst[768:1152, 256:768]
    total = dot_t(back, high) + dot_t(back, low)
    total = total + sfine[...].reshape(16, 32, 256)[:, 0:24].reshape(384, 256)
    sfine_own = total

    for copy in three:
        copy.wait_recv()
    top = (dmat[variant] + rmat[2]) + (rmat[0] + rmat[1])
    mid = interleave(top[2:8], widen(top[1:10], 6))
    mid = trimmed(mid)
    fine = interleave(mid[2:10], widen(mid[1:12], 8))
    lower = lax.broadcasted_iota(jnp.int32, (16, 8, 128), 2) < 64
    fine = jnp.concatenate(
        [jnp.where(lower, fine, 0.0), jnp.where(lower, 0.0, fine)], axis=1
    ).reshape(256, 128)
    high, low = split(fine)
    up_high, up_low = cst[0:384, 384:512], cst[0:384, 512:640]
    result = dot_t(up_high, high) + (dot_t(up_high, low) + dot_t(up_low, high)) + sfine_own
    out_ref[...] = result.reshape(16, 24, 256)

    for copy in one + [cross_x] + two + [cross_m] + three:
        copy.wait_send()

    @pl.loop(1, nz)
    def _(d):
        gather(d, gz).wait_send()


def solution(mesh):
    whole, spread = constants()
    nz = mesh.shape["gz"]
    vmem = pl.BlockSpec(memory_space=pltpu.VMEM)
    smem = pl.BlockSpec(memory_space=pltpu.SMEM)
    dma = pltpu.SemaphoreType.DMA

    def per_device(charges, kernel_fine, kernel_mid, gauss_width, gauss_weight):
        return pl.pallas_call(
            kernel,
            out_shape=jax.ShapeDtypeStruct((16, 24, 256), F32),
            in_specs=[vmem, vmem, vmem, smem, smem, pl.BlockSpec(memory_space=pl.ANY), vmem],
            out_specs=vmem,
            scratch_shapes=[
                pltpu.VMEM((ROWS_C, 768), BF16),
                pltpu.VMEM((24, 16, 768), BF16),
                pltpu.VMEM((16, 16, 128), BF16),
                pltpu.VMEM((24, 16, 256), BF16),
                pltpu.VMEM((384, 768), BF16),
                pltpu.VMEM((9, 256, 512), BF16),
                pltpu.VMEM((9, 256, 512), BF16),
                pltpu.VMEM((20, 16, 512), BF16),
                pltpu.VMEM((320, 768), BF16),
                pltpu.VMEM((nz, 8, 512), F32),
                pltpu.VMEM((2, 256, 256), F32),
                pltpu.VMEM((192, 512), F32),
                pltpu.VMEM((256, 256), F32),
                pltpu.VMEM((4, 10, 8, 128), F32),
                pltpu.VMEM((3, 10, 8, 128), F32),
                pltpu.VMEM((2, 128, 256), BF16),
                pltpu.VMEM((2, 256, 512), BF16),
                pltpu.VMEM((2, 256, 512), BF16),
                dma((2,)),
                dma((6,)), dma((6,)),
                dma((6,)), dma((6,)),
                dma((nz,)), dma((nz,)),
                dma((3,)), dma((3,)),
            ],
            compiler_params=pltpu.CompilerParams(
                collective_id=0, has_side_effects=True, vmem_limit_bytes=48 * 2**20
            ),
        )(
            charges, kernel_fine, kernel_mid, gauss_width, gauss_weight,
            jnp.asarray(whole), jnp.asarray(spread),
        )

    placed = (P("gx", "gy", "gz"), P(), P(), P(), P())
    return jax.shard_map(
        per_device, mesh=mesh, in_specs=placed, out_specs=P("gx", "gy", "gz"), check_vma=False
    )
```

```python
import jax
import jax.numpy as jnp
import numpy as np
import ml_dtypes
from jax import lax
from jax.experimental import pallas as pl
from jax.experimental.pallas import tpu as pltpu
from jax.sharding import PartitionSpec as P

M = 16
GAUSS = 8
MESH = pl.DeviceIdType.MESH
F32 = jnp.float32
BF16 = jnp.bfloat16


def weight(offset):
    return {0: 1.0, 1: 9 / 16, 3: -1 / 16}.get(abs(offset), 0.0)


def halo_list(side, size):
    if side == 0:
        return [size, size + 1, size + 2, size + 3, size + 5, None, None, None]
    return [-9, -7, -6, -5, -4, -3, -2, -1]


def extra_list(side, size):
    return [size + 1] if side == 0 else [-3, -1]


def cross(xs, ys):
    return [None if (x is None or y is None) else (x, y) for x in xs for y in ys]


def moved(coords, dx, dy):
    return [None if c is None else (c[0] + dx, c[1] + dy) for c in coords]


def padded(coords, size):
    return coords + [None] * (size - len(coords))


def picker(source, target):
    where = {c: i for i, c in enumerate(source) if c is not None}
    table = np.zeros((len(source), len(target)), np.float32)
    for j, c in enumerate(target):
        if c in where:
            table[where[c], j] = 1.0
    return table


def weights_between(fine, coarse):
    table = np.zeros((len(fine), len(coarse)), np.float32)
    for i, f in enumerate(fine):
        if f is None:
            continue
        for j, c in enumerate(coarse):
            if c is not None:
                table[i, j] = weight(f[0] - 2 * c[0]) * weight(f[1] - 2 * c[1])
    return table


ROWS_A = 512
ROWS_C = 2560


def plane(gx, gy):
    yl, xl = halo_list(gy, 24), halo_list(gx, 16)
    own = cross(range(16), range(24))
    fine = own + cross(range(16), yl) + cross(xl, list(range(24)) + yl)
    mid_own = cross(range(8), range(12))
    xs = list(range(8)) + extra_list(gx, 8)
    ys = list(range(12)) + extra_list(gy, 12)
    extra = [c for c in cross(xs, ys) if c not in set(mid_own)]
    mid = padded(mid_own, 128) + padded(extra, 128)
    return own, fine, mid_own, mid


def constants():
    whole = np.zeros((4, ROWS_C, 768), np.float32)
    spread = np.full((4, 32, 512), 1e30, np.float32)
    for gx in range(2):
        for gy in range(2):
            v = gx * 2 + gy
            own, fine, mid_own, mid = plane(gx, gy)
            out = whole[v]
            dy = 24 if gy == 0 else -24
            dx = 16 if gx == 0 else -16
            other_y = plane(gx, 1 - gy)[1]
            other_x = plane(1 - gx, gy)[1]
            out[0:384, 256:384] = picker(own, moved(other_y[384:512], 0, dy))
            out[0:512, 0:256] = picker(fine[:512], moved(other_x[512:768], dx, 0))
            xs = range(0, 7) if gx == 0 else range(-3, 4)
            ys = range(0, 9) if gy == 0 else range(-3, 6)
            window = padded(cross(xs, ys), 64)
            inside = cross(
                range(0, 10) if gx == 0 else range(-2, 8), range(0, 14) if gy == 0 else range(-2, 12)
            )
            up = weights_between(own, inside).astype(np.float64) @ weights_between(inside, window)
            up = np.concatenate([up, up], axis=1)
            high = up.astype(ml_dtypes.bfloat16).astype(np.float64)
            out[0:384, 384:512] = high
            out[0:384, 512:640] = up - high
            rz = np.zeros((256, 128), np.float32)
            for j in range(256):
                for i in range(128):
                    rz[j, i] = weight(j - 2 * i)
            out[0:256, 640:768] = rz
            out[512:1280, 0:256] = weights_between(fine, mid)
            top = padded(cross(range(4), range(6)), 32)
            out[512:768, 256:768] = np.tile(weights_between(mid, top), (1, 16))
            lanes = [c if c in set(inside) else None for c in cross(range(-2, 14), range(-2, 30))]
            out[768:1152, 256:768] = weights_between(own, lanes)
            out[1280:2048] = picker(fine, cross(range(-4, 20), range(-4, 28)))
            blocks = []
            for bx in (0, dx // 2):
                for by in (0, dy // 2):
                    blocks += padded(moved(mid_own, bx, by), 128)
            out[2048:2560] = picker(blocks, cross(range(-6, 18), range(-6, 26)))
            for i, c in enumerate(top):
                if c is None:
                    continue
                for wx in range(2):
                    for wy in range(2):
                        for xi in range(7):
                            for yi in range(9):
                                d = (4 * gx + c[0] - wx - xi) ** 2 + (6 * gy + c[1] - 3 * wy - yi) ** 2
                                lane = (wx * 2 + wy) * 128 + xi * 9 + yi
                                spread[v, i, lane] = d
                                spread[v, i, lane + 64] = d
    return whole.astype(ml_dtypes.bfloat16), spread


def dot(a, b):
    return lax.dot_general(a, b, (((1,), (0,)), ((), ())), preferred_element_type=F32)


def dot_t(a, b):
    return lax.dot_general(a, b, (((1,), (1,)), ((), ())), preferred_element_type=F32)


def split(a):
    high = a.astype(BF16)
    return high, (a - high.astype(F32)).astype(BF16)


def widen(a, count):
    near, far = 9.0 / 16.0, -1.0 / 16.0
    odd = near * (a[1 : count + 1] + a[2 : count + 2]) + far * (a[0:count] + a[3 : count + 3])
    return odd


def interleave(even, odd):
    both = jnp.concatenate([even[:, None], odd[:, None]], axis=1)
    return both.reshape((2 * even.shape[0],) + even.shape[1:])


def kernel(
    q_hbm, kf_hbm, km_hbm, gw_hbm, gg_hbm, cst_hbm, spread_hbm, out_ref,
    q_ref, kf_ref, km_ref, gw_ref, gg_ref, spread_ref, base, cst, fq, py, px, fpad, tfine, tmid, fm, mpad, gath, sfine, smid, amat, dmat, rmat, ezr, wlo, whi,
    cst_sem, s1, r1, s2, r2, sg, rg, s3, r3,
):
    gx, gy, gz = lax.axis_index("gx"), lax.axis_index("gy"), lax.axis_index("gz")
    nz = lax.axis_size("gz")
    ox, oy = 1 - gx, 1 - gy
    up, down = lax.rem(gz + 1, nz), lax.rem(gz + nz - 1, nz)
    variant = gx * 2 + gy

    first = pltpu.make_async_copy(
        cst_hbm.at[variant, pl.ds(0, ROWS_A)], cst.at[pl.ds(0, ROWS_A)], cst_sem.at[0]
    )
    rest = pltpu.make_async_copy(
        cst_hbm.at[variant, pl.ds(ROWS_A, ROWS_C - ROWS_A)],
        cst.at[pl.ds(ROWS_A, ROWS_C - ROWS_A)],
        cst_sem.at[1],
    )
    inputs = [
        pltpu.make_async_copy(src, dst, cst_sem.at[2 + i])
        for i, (src, dst) in enumerate(
            (
                (q_hbm, q_ref), (kf_hbm, kf_ref), (km_hbm, km_ref), (gw_hbm, gw_ref),
                (gg_hbm, gg_ref), (spread_hbm.at[variant], spread_ref),
            )
        )
    ]
    for copy in inputs[:2]:
        copy.start()
    first.start()
    for copy in inputs[2:]:
        copy.start()
    rest.start()

    barrier = pltpu.get_barrier_semaphore()
    for peer in ((ox, gy, gz), (gx, oy, gz), (ox, oy, gz), (gx, oy, up), (gx, oy, down)):
        pl.semaphore_signal(barrier, inc=1, device_id=peer, device_id_type=MESH)

    @pl.loop(1, nz)
    def _(d):
        pl.semaphore_signal(
            barrier, inc=1, device_id=(gx, gy, lax.rem(gz + d, nz)), device_id_type=MESH
        )

    inputs[0].wait()
    turned = q_ref[...].astype(F32).reshape(384, 256).T.astype(BF16)
    fq[4:20, :, 0:384] = turned.reshape(16, 16, 384)
    first.wait()
    py[...] = dot(turned, cst[0:384, 256:384]).astype(BF16).reshape(16, 16, 128)

    def build(k_ref, table):
        lane = lax.broadcasted_iota(jnp.int32, (9, 512), 1)
        row = lax.broadcasted_iota(jnp.int32, (9, 512), 0)
        total = jnp.zeros((9, 512), F32)
        for a in range(9):
            place = (lane == row + 32 * a).astype(F32).astype(BF16)
            total = total + lax.dot_general(
                k_ref[a], place, (((0,), (0,)), ((), ())), preferred_element_type=F32
            )
        base[0:9] = total

        @pl.loop(0, 9)
        def _(c):
            line = jnp.broadcast_to(base[pl.ds(c, 1)], (16, 512))
            strip = pltpu.roll(line, 0, 1, stride=1, stride_axis=0)
            for i in range(8):
                part = pltpu.roll(strip, 16 * i, 1).astype(BF16)
                table[c, 16 * i : 16 * i + 16, :] = part
                table[c, 128 + 16 * i : 144 + 16 * i, 0:128] = part[:, 384:512]
                table[c, 128 + 16 * i : 144 + 16 * i, 128:512] = part[:, 0:384]

    inputs[1].wait()
    build(kf_ref, tfine)

    pl.semaphore_wait(barrier, nz - 1 + 5)

    def send(src, dst, sems, recvs, i, peer):
        copy = pltpu.make_async_remote_copy(
            src_ref=src, dst_ref=dst, send_sem=sems.at[i], recv_sem=recvs.at[i],
            device_id=peer, device_id_type=MESH,
        )
        copy.start()
        return copy

    ways = [
        (py.at[12:16], fq.at[0:4, :, 384:512], (gx, oy, up)),
        (py.at[0:4], fq.at[20:24, :, 384:512], (gx, oy, down)),
        (fq.at[16:20, :, 0:384], fq.at[0:4, :, 0:384], (gx, gy, up)),
        (fq.at[4:8, :, 0:384], fq.at[20:24, :, 0:384], (gx, gy, down)),
        (py, fq.at[4:20, :, 384:512], (gx, oy, gz)),
    ]
    one = [send(src, dst, s1, r1, i, peer) for i, (src, dst, peer) in enumerate(ways)]

    for copy in inputs[2:]:
        copy.wait()
    build(km_ref, tmid)
    rest.wait()
    node = gz * 4 - 3 + lax.broadcasted_iota(jnp.int32, (16, 128), 0)
    gap = (node - lax.broadcasted_iota(jnp.int32, (16, 128), 1)).astype(F32)
    exists = (node >= 0) & (node < 4 * nz)
    half = lax.rem(lax.broadcasted_iota(jnp.int32, (32, 512), 1), 128) < 64
    parts = []
    for g in range(GAUSS):
        width = jnp.full((16, 128), gw_ref[g], F32)
        ratio = gap / width
        parts.append(jnp.where(exists, jnp.exp(-(ratio * ratio)) / jnp.sqrt(width), 0.0))
        width = jnp.full((32, 512), gw_ref[g], F32)
        both = jnp.exp(-(spread_ref[...] / (width * width))) * (gg_ref[g] / width)
        for table, keep in ((wlo, half), (whi, jnp.logical_not(half))):
            high, low = split(jnp.where(keep, both, 0.0))
            table[0, 32 * g : 32 * g + 32] = high
            table[1, 32 * g : 32 * g + 32] = low
    ez = jnp.concatenate(parts, axis=0)
    rz = cst[0:256, 640:768]
    high, low = split(ez)
    low2 = (ez - high.astype(F32) - low.astype(F32)).astype(BF16)
    high, low = split(dot_t(high, rz) + dot_t(low, rz) + dot_t(low2, rz))
    ezr[0] = high
    ezr[1] = low

    for copy in one:
        copy.wait_recv()
    keep_low = (gz > 0).astype(F32).astype(BF16)
    keep_high = (gz < nz - 1).astype(F32).astype(BF16)
    fq[0:4, :, 0:512] = fq[0:4, :, 0:512] * keep_low
    fq[20:24, :, 0:512] = fq[20:24, :, 0:512] * keep_high
    known = fq[:, :, 0:512].reshape(384, 512)
    px[...] = dot(known, cst[0:512, 0:256]).astype(BF16).reshape(24, 16, 256)
    cross_x = send(px, fq.at[:, :, 512:768], s1, r1, 5, (ox, gy, gz))
    plane_mid = dot(known, cst[512:1024, 0:256])
    cross_x.wait_recv()
    plane_mid = plane_mid + dot(fq[:, :, 512:768].reshape(384, 256), cst[1024:1280, 0:256])
    rows = plane_mid.reshape(12, 2, 16, 256)
    even, odd = rows[:, 0], rows[:, 1]
    q_mid = (
        even[2:10]
        + (9.0 / 16.0) * (odd[1:9] + odd[2:10])
        + (-1.0 / 16.0) * (odd[0:8] + odd[3:11])
    ).astype(BF16)
    fm[6:14, :, 0:128] = q_mid[:, :, 0:128]
    tops = dot(q_mid.reshape(128, 256), cst[512:768, 256:768]).reshape(8, 16, 512)
    member = lax.broadcasted_iota(jnp.int32, (16, 512), 0)
    group = lax.broadcasted_iota(jnp.int32, (16, 512), 1) // 32
    gath[gz] = jnp.sum(jnp.where((member == group)[None], tops, 0.0), axis=1)

    def gather(d, slot):
        return pltpu.make_async_remote_copy(
            src_ref=gath.at[slot], dst_ref=gath.at[slot], send_sem=sg.at[d], recv_sem=rg.at[slot],
            device_id=(gx, gy, lax.rem(gz + d, nz)), device_id_type=MESH,
        )

    @pl.loop(1, nz)
    def _(d):
        gather(d, gz).start()

    ways = [
        (fm.at[8:14, :, 0:128], fm.at[0:6, :, 128:256], (gx, oy, up)),
        (fm.at[6:12, :, 0:128], fm.at[14:20, :, 128:256], (gx, oy, down)),
        (fm.at[8:14, :, 0:128], fm.at[0:6, :, 0:128], (gx, gy, up)),
        (fm.at[6:12, :, 0:128], fm.at[14:20, :, 0:128], (gx, gy, down)),
        (fm.at[6:14, :, 0:128], fm.at[6:14, :, 128:256], (gx, oy, gz)),
    ]
    two = [send(src, dst, s2, r2, i, peer) for i, (src, dst, peer) in enumerate(ways)]

    fpad[...] = dot(fq[...].reshape(384, 768), cst[1280:2048, :]).astype(BF16)
    for g in range(2):
        total = None
        for c in range(9):
            term = dot_t(tfine[c], fpad[16 * c : 16 * c + 256, 256 * g : 256 * g + 512])
            total = term if total is None else total + term
        sfine[g] = total

    for copy in two:
        copy.wait_recv()
    fm[0:6, :, 0:256] = fm[0:6, :, 0:256] * keep_low
    fm[14:20, :, 0:256] = fm[14:20, :, 0:256] * keep_high
    cross_m = send(fm.at[:, :, 0:256], fm.at[:, :, 256:512], s2, r2, 5, (ox, gy, gz))

    @pl.loop(1, nz)
    def _(d):
        gather(d, lax.rem(gz + nz - d, nz)).wait_recv()

    high, low = split(gath[...].reshape(256, 512))
    fields = dot(ezr[0], high) + (dot(ezr[0], low) + dot(ezr[1], high))
    lane = lax.broadcasted_iota(jnp.int32, (16, 128), 1) // 32
    for j in range(4):
        tile = fields[:, 128 * j : 128 * j + 128]
        turns = [tile] + [pltpu.roll(tile, 32 * t, 1) for t in range(1, 4)]
        for i in range(4):
            m = 4 * j + i
            for t in range(2):
                block = None
                for s in range(4):
                    g = 4 * t + s
                    piece = turns[(s - i) % 4][16 * g : 16 * g + 16]
                    block = piece if block is None else jnp.where(lane == s, piece, block)
                amat[16 * m : 16 * m + 16, 128 * t : 128 * t + 128] = block
    high, low = split(amat[...])
    share = dot(high[0:128], wlo[0]) + dot(high[128:256], whi[0])
    share = share + (dot(low[0:128], wlo[0]) + dot(low[128:256], whi[0]))
    share = share + (dot(high[0:128], wlo[1]) + dot(high[128:256], whi[1]))
    share = jnp.swapaxes(share.reshape(8, 16, 512), 0, 1)
    for w in range(4):
        dmat[w] = share[0:10, :, 128 * w : 128 * w + 128]
    ways = [(oy + 2 * gx, (gx, oy, gz)), (oy + 2 * ox, (ox, oy, gz)), (gy + 2 * ox, (ox, gy, gz))]
    three = [send(dmat.at[w], rmat.at[i], s3, r3, i, peer) for i, (w, peer) in enumerate(ways)]

    cross_m.wait_recv()
    mpad[...] = dot(fm[...].reshape(320, 512), cst[2048:2560, :]).astype(BF16)
    for g in range(2):
        total = None
        for c in range(9):
            term = dot_t(mpad[16 * c : 16 * c + 192, 256 * g : 256 * g + 512], tmid[c])
            total = term if total is None else total + term
        smid[:, 256 * g : 256 * g + 256] = total

    def trimmed(mid):
        spot = lax.broadcasted_iota(jnp.int32, mid.shape, 0) - 2 + 8 * gz
        return jnp.where((spot >= 0) & (spot < 8 * nz), mid, 0.0)

    mid = trimmed(smid[...].reshape(12, 16, 512))
    fine = interleave(mid[2:10], widen(mid[1:12], 8)).reshape(256, 512)
    high, low = split(fine)
    back = cst[768:1152, 256:768]
    total = dot_t(back, high) + dot_t(back, low)
    total = total + sfine[...].reshape(16, 32, 256)[:, 0:24].reshape(384, 256)
    sfine_own = total

    for copy in three:
        copy.wait_recv()
    top = (dmat[variant] + rmat[2]) + (rmat[0] + rmat[1])
    mid = interleave(top[2:8], widen(top[1:10], 6))
    mid = trimmed(mid)
    fine = interleave(mid[2:10], widen(mid[1:12], 8))
    lower = lax.broadcasted_iota(jnp.int32, (16, 8, 128), 2) < 64
    fine = jnp.concatenate(
        [jnp.where(lower, fine, 0.0), jnp.where(lower, 0.0, fine)], axis=1
    ).reshape(256, 128)
    high, low = split(fine)
    up_high, up_low = cst[0:384, 384:512], cst[0:384, 512:640]
    result = dot_t(up_high, high) + (dot_t(up_high, low) + dot_t(up_low, high)) + sfine_own
    out_ref[...] = result.reshape(16, 24, 256)

    for copy in one + [cross_x] + two + [cross_m] + three:
        copy.wait_send()

    @pl.loop(1, nz)
    def _(d):
        gather(d, gz).wait_send()


def solution(mesh):
    whole, spread = constants()
    nz = mesh.shape["gz"]
    vmem = pl.BlockSpec(memory_space=pltpu.VMEM)
    dma = pltpu.SemaphoreType.DMA

    def per_device(charges, kernel_fine, kernel_mid, gauss_width, gauss_weight):
        return pl.pallas_call(
            kernel,
            out_shape=jax.ShapeDtypeStruct((16, 24, 256), F32),
            in_specs=[pl.BlockSpec(memory_space=pltpu.HBM)] * 7,
            out_specs=vmem,
            scratch_shapes=[
                pltpu.VMEM((16, 24, 256), BF16),
                pltpu.VMEM((9, 9, 9), BF16),
                pltpu.VMEM((9, 9, 9), BF16),
                pltpu.SMEM((GAUSS,), F32),
                pltpu.SMEM((GAUSS,), F32),
                pltpu.VMEM((32, 512), F32),
                pltpu.VMEM((16, 512), F32),
                pltpu.VMEM((ROWS_C, 768), BF16),
                pltpu.VMEM((24, 16, 768), BF16),
                pltpu.VMEM((16, 16, 128), BF16),
                pltpu.VMEM((24, 16, 256), BF16),
                pltpu.VMEM((384, 768), BF16),
                pltpu.VMEM((9, 256, 512), BF16),
                pltpu.VMEM((9, 256, 512), BF16),
                pltpu.VMEM((20, 16, 512), BF16),
                pltpu.VMEM((320, 768), BF16),
                pltpu.VMEM((nz, 8, 512), F32),
                pltpu.VMEM((2, 256, 256), F32),
                pltpu.VMEM((192, 512), F32),
                pltpu.VMEM((256, 256), F32),
                pltpu.VMEM((4, 10, 8, 128), F32),
                pltpu.VMEM((3, 10, 8, 128), F32),
                pltpu.VMEM((2, 128, 256), BF16),
                pltpu.VMEM((2, 256, 512), BF16),
                pltpu.VMEM((2, 256, 512), BF16),
                dma((8,)),
                dma((6,)), dma((6,)),
                dma((6,)), dma((6,)),
                dma((nz,)), dma((nz,)),
                dma((3,)), dma((3,)),
            ],
            compiler_params=pltpu.CompilerParams(
                collective_id=0, has_side_effects=True, vmem_limit_bytes=48 * 2**20
            ),
        )(
            charges, kernel_fine, kernel_mid, gauss_width, gauss_weight,
            jnp.asarray(whole), jnp.asarray(spread),
        )

    placed = (P("gx", "gy", "gz"), P(), P(), P(), P())
    return jax.shard_map(
        per_device, mesh=mesh, in_specs=placed, out_specs=P("gx", "gy", "gz"), check_vma=False
    )
```

```python
import jax
import jax.numpy as jnp
import numpy as np
import ml_dtypes
from jax import lax
from jax.experimental import pallas as pl
from jax.experimental.pallas import tpu as pltpu
from jax.sharding import PartitionSpec as P

M = 16
GAUSS = 8
MESH = pl.DeviceIdType.MESH
F32 = jnp.float32
BF16 = jnp.bfloat16


def weight(offset):
    return {0: 1.0, 1: 9 / 16, 3: -1 / 16}.get(abs(offset), 0.0)


def halo_list(side, size):
    if side == 0:
        return [size, size + 1, size + 2, size + 3, size + 5, None, None, None]
    return [-9, -7, -6, -5, -4, -3, -2, -1]


def extra_list(side, size):
    return [size + 1] if side == 0 else [-3, -1]


def cross(xs, ys):
    return [None if (x is None or y is None) else (x, y) for x in xs for y in ys]


def moved(coords, dx, dy):
    return [None if c is None else (c[0] + dx, c[1] + dy) for c in coords]


def padded(coords, size):
    return coords + [None] * (size - len(coords))


def picker(source, target):
    where = {c: i for i, c in enumerate(source) if c is not None}
    table = np.zeros((len(source), len(target)), np.float32)
    for j, c in enumerate(target):
        if c in where:
            table[where[c], j] = 1.0
    return table


def weights_between(fine, coarse):
    table = np.zeros((len(fine), len(coarse)), np.float32)
    for i, f in enumerate(fine):
        if f is None:
            continue
        for j, c in enumerate(coarse):
            if c is not None:
                table[i, j] = weight(f[0] - 2 * c[0]) * weight(f[1] - 2 * c[1])
    return table


ROWS_A = 512
ROWS_C = 2560


def plane(gx, gy):
    yl, xl = halo_list(gy, 24), halo_list(gx, 16)
    own = cross(range(16), range(24))
    fine = own + cross(range(16), yl) + cross(xl, list(range(24)) + yl)
    mid_own = cross(range(8), range(12))
    xs = list(range(8)) + extra_list(gx, 8)
    ys = list(range(12)) + extra_list(gy, 12)
    extra = [c for c in cross(xs, ys) if c not in set(mid_own)]
    mid = padded(mid_own, 128) + padded(extra, 128)
    return own, fine, mid_own, mid


def constants():
    whole = np.zeros((4, ROWS_C, 768), np.float32)
    spread = np.full((4, 32, 512), 1e30, np.float32)
    for gx in range(2):
        for gy in range(2):
            v = gx * 2 + gy
            own, fine, mid_own, mid = plane(gx, gy)
            out = whole[v]
            dy = 24 if gy == 0 else -24
            dx = 16 if gx == 0 else -16
            other_y = plane(gx, 1 - gy)[1]
            other_x = plane(1 - gx, gy)[1]
            out[0:384, 256:384] = picker(own, moved(other_y[384:512], 0, dy))
            out[0:512, 0:256] = picker(fine[:512], moved(other_x[512:768], dx, 0))
            xs = range(0, 7) if gx == 0 else range(-3, 4)
            ys = range(0, 9) if gy == 0 else range(-3, 6)
            window = padded(cross(xs, ys), 64)
            inside = cross(
                range(0, 10) if gx == 0 else range(-2, 8), range(0, 14) if gy == 0 else range(-2, 12)
            )
            up = weights_between(own, inside).astype(np.float64) @ weights_between(inside, window)
            up = np.concatenate([up, up], axis=1)
            high = up.astype(ml_dtypes.bfloat16).astype(np.float64)
            out[0:384, 384:512] = high
            out[0:384, 512:640] = up - high
            rz = np.zeros((256, 128), np.float32)
            for j in range(256):
                for i in range(128):
                    rz[j, i] = weight(j - 2 * i)
            out[0:256, 640:768] = rz
            out[512:1280, 0:256] = weights_between(fine, mid)
            top = padded(cross(range(4), range(6)), 32)
            out[512:768, 256:768] = np.tile(weights_between(mid, top), (1, 16))
            lanes = [c if c in set(inside) else None for c in cross(range(-2, 14), range(-2, 30))]
            out[768:1152, 256:768] = weights_between(own, lanes)
            out[1280:2048] = picker(fine, cross(range(-4, 20), range(-4, 28)))
            blocks = []
            for bx in (0, dx // 2):
                for by in (0, dy // 2):
                    blocks += padded(moved(mid_own, bx, by), 128)
            out[2048:2560] = picker(blocks, cross(range(-6, 18), range(-6, 26)))
            for i, c in enumerate(top):
                if c is None:
                    continue
                for wx in range(2):
                    for wy in range(2):
                        for xi in range(7):
                            for yi in range(9):
                                d = (4 * gx + c[0] - wx - xi) ** 2 + (6 * gy + c[1] - 3 * wy - yi) ** 2
                                lane = (wx * 2 + wy) * 128 + xi * 9 + yi
                                spread[v, i, lane] = d
                                spread[v, i, lane + 64] = d
    return whole.astype(ml_dtypes.bfloat16), spread


def dot(a, b):
    return lax.dot_general(a, b, (((1,), (0,)), ((), ())), preferred_element_type=F32)


def dot_t(a, b):
    return lax.dot_general(a, b, (((1,), (1,)), ((), ())), preferred_element_type=F32)


def split(a):
    high = a.astype(BF16)
    return high, (a - high.astype(F32)).astype(BF16)


def widen(a, count):
    near, far = 9.0 / 16.0, -1.0 / 16.0
    odd = near * (a[1 : count + 1] + a[2 : count + 2]) + far * (a[0:count] + a[3 : count + 3])
    return odd


def interleave(even, odd):
    both = jnp.concatenate([even[:, None], odd[:, None]], axis=1)
    return both.reshape((2 * even.shape[0],) + even.shape[1:])


def kernel(
    q_hbm, kf_hbm, km_hbm, gw_hbm, gg_hbm, cst_hbm, spread_hbm, out_ref,
    q_ref, kf_ref, km_ref, gw_ref, gg_ref, spread_ref, base, cst, fq, py, px, fpad, tfine, tmid, fm, mpad, gath, sfine, smid, amat, dmat, rmat, ezr, wlo, whi,
    cst_sem, s1, r1, s2, r2, sg, rg, s3, r3,
):
    gx, gy, gz = lax.axis_index("gx"), lax.axis_index("gy"), lax.axis_index("gz")
    nz = lax.axis_size("gz")
    ox, oy = 1 - gx, 1 - gy
    up, down = lax.rem(gz + 1, nz), lax.rem(gz + nz - 1, nz)
    variant = gx * 2 + gy

    first = pltpu.make_async_copy(
        cst_hbm.at[variant, pl.ds(0, ROWS_A)], cst.at[pl.ds(0, ROWS_A)], cst_sem.at[0]
    )
    rest = pltpu.make_async_copy(
        cst_hbm.at[variant, pl.ds(ROWS_A, ROWS_C - ROWS_A)],
        cst.at[pl.ds(ROWS_A, ROWS_C - ROWS_A)],
        cst_sem.at[1],
    )
    inputs = [
        pltpu.make_async_copy(src, dst, cst_sem.at[2 + i])
        for i, (src, dst) in enumerate(
            (
                (q_hbm, q_ref), (kf_hbm, kf_ref), (km_hbm, km_ref), (gw_hbm, gw_ref),
                (gg_hbm, gg_ref), (spread_hbm.at[variant], spread_ref),
            )
        )
    ]
    for copy in inputs[:2]:
        copy.start()
    first.start()
    for copy in inputs[2:]:
        copy.start()
    rest.start()

    barrier = pltpu.get_barrier_semaphore()
    for peer in ((ox, gy, gz), (gx, oy, gz), (ox, oy, gz), (gx, oy, up), (gx, oy, down)):
        pl.semaphore_signal(barrier, inc=1, device_id=peer, device_id_type=MESH)

    @pl.loop(1, nz)
    def _(d):
        pl.semaphore_signal(
            barrier, inc=1, device_id=(gx, gy, lax.rem(gz + d, nz)), device_id_type=MESH
        )

    inputs[0].wait()
    turned = q_ref[...].astype(F32).reshape(384, 256).T.astype(BF16)
    fq[4:20, :, 0:384] = turned.reshape(16, 16, 384)
    first.wait()
    py[...] = dot(turned, cst[0:384, 256:384]).astype(BF16).reshape(16, 16, 128)

    def build(k_ref, table):
        lane = lax.broadcasted_iota(jnp.int32, (9, 512), 1)
        row = lax.broadcasted_iota(jnp.int32, (9, 512), 0)
        total = jnp.zeros((9, 512), F32)
        for a in range(9):
            place = (lane == row + 32 * a).astype(F32).astype(BF16)
            total = total + lax.dot_general(
                k_ref[a], place, (((0,), (0,)), ((), ())), preferred_element_type=F32
            )
        base[0:9] = total

        @pl.loop(0, 9)
        def _(c):
            line = jnp.broadcast_to(base[pl.ds(c, 1)], (16, 512))
            strip = pltpu.roll(line, 0, 1, stride=1, stride_axis=0)
            for i in range(8):
                part = pltpu.roll(strip, 16 * i, 1).astype(BF16)
                table[c, 16 * i : 16 * i + 16, :] = part
                table[c, 128 + 16 * i : 144 + 16 * i, 0:128] = part[:, 384:512]
                table[c, 128 + 16 * i : 144 + 16 * i, 128:512] = part[:, 0:384]

    inputs[1].wait()
    build(kf_ref, tfine)

    pl.semaphore_wait(barrier, nz - 1 + 5)

    def send(src, dst, sems, recvs, i, peer):
        copy = pltpu.make_async_remote_copy(
            src_ref=src, dst_ref=dst, send_sem=sems.at[i], recv_sem=recvs.at[i],
            device_id=peer, device_id_type=MESH,
        )
        copy.start()
        return copy

    ways = [
        (py.at[12:16], fq.at[0:4, :, 384:512], (gx, oy, up)),
        (py.at[0:4], fq.at[20:24, :, 384:512], (gx, oy, down)),
        (fq.at[16:20, :, 0:384], fq.at[0:4, :, 0:384], (gx, gy, up)),
        (fq.at[4:8, :, 0:384], fq.at[20:24, :, 0:384], (gx, gy, down)),
        (py, fq.at[4:20, :, 384:512], (gx, oy, gz)),
    ]
    one = [send(src, dst, s1, r1, i, peer) for i, (src, dst, peer) in enumerate(ways)]

    for copy in inputs[2:]:
        copy.wait()
    build(km_ref, tmid)
    rest.wait()
    node = gz * 4 - 3 + lax.broadcasted_iota(jnp.int32, (16, 128), 0)
    gap = (node - lax.broadcasted_iota(jnp.int32, (16, 128), 1)).astype(F32)
    exists = (node >= 0) & (node < 4 * nz)
    half = lax.rem(lax.broadcasted_iota(jnp.int32, (32, 512), 1), 128) < 64
    parts = []
    for g in range(GAUSS):
        width = jnp.full((16, 128), gw_ref[g], F32)
        ratio = gap / width
        parts.append(jnp.where(exists, jnp.exp(-(ratio * ratio)) / jnp.sqrt(width), 0.0))
        width = jnp.full((32, 512), gw_ref[g], F32)
        both = jnp.exp(-(spread_ref[...] / (width * width))) * (gg_ref[g] / width)
        for table, keep in ((wlo, half), (whi, jnp.logical_not(half))):
            high, low = split(jnp.where(keep, both, 0.0))
            table[0, 32 * g : 32 * g + 32] = high
            table[1, 32 * g : 32 * g + 32] = low
    ez = jnp.concatenate(parts, axis=0)
    rz = cst[0:256, 640:768]
    high, low = split(ez)
    low2 = (ez - high.astype(F32) - low.astype(F32)).astype(BF16)
    high, low = split(dot_t(high, rz) + dot_t(low, rz) + dot_t(low2, rz))
    ezr[0] = high
    ezr[1] = low

    for copy in one:
        copy.wait_recv()
    keep_low = (gz > 0).astype(F32).astype(BF16)
    keep_high = (gz < nz - 1).astype(F32).astype(BF16)
    fq[0:4, :, 0:512] = fq[0:4, :, 0:512] * keep_low
    fq[20:24, :, 0:512] = fq[20:24, :, 0:512] * keep_high
    known = fq[:, :, 0:512].reshape(384, 512)
    px[...] = dot(known, cst[0:512, 0:256]).astype(BF16).reshape(24, 16, 256)
    cross_x = send(px, fq.at[:, :, 512:768], s1, r1, 5, (ox, gy, gz))
    plane_mid = dot(known, cst[512:1024, 0:256])
    cross_x.wait_recv()
    plane_mid = plane_mid + dot(fq[:, :, 512:768].reshape(384, 256), cst[1024:1280, 0:256])
    rows = plane_mid.reshape(12, 2, 16, 256)
    even, odd = rows[:, 0], rows[:, 1]
    q_mid = (
        even[2:10]
        + (9.0 / 16.0) * (odd[1:9] + odd[2:10])
        + (-1.0 / 16.0) * (odd[0:8] + odd[3:11])
    ).astype(BF16)
    fm[6:14, :, 0:128] = q_mid[:, :, 0:128]
    tops = dot(q_mid.reshape(128, 256), cst[512:768, 256:768]).reshape(8, 16, 512)
    member = lax.broadcasted_iota(jnp.int32, (16, 512), 0)
    group = lax.broadcasted_iota(jnp.int32, (16, 512), 1) // 32
    gath[gz] = jnp.sum(jnp.where((member == group)[None], tops, 0.0), axis=1)

    def gather(d, slot):
        return pltpu.make_async_remote_copy(
            src_ref=gath.at[slot], dst_ref=gath.at[slot], send_sem=sg.at[d], recv_sem=rg.at[slot],
            device_id=(gx, gy, lax.rem(gz + d, nz)), device_id_type=MESH,
        )

    @pl.loop(1, nz)
    def _(d):
        gather(d, gz).start()

    ways = [
        (fm.at[8:14, :, 0:128], fm.at[0:6, :, 128:256], (gx, oy, up)),
        (fm.at[6:12, :, 0:128], fm.at[14:20, :, 128:256], (gx, oy, down)),
        (fm.at[8:14, :, 0:128], fm.at[0:6, :, 0:128], (gx, gy, up)),
        (fm.at[6:12, :, 0:128], fm.at[14:20, :, 0:128], (gx, gy, down)),
        (fm.at[6:14, :, 0:128], fm.at[6:14, :, 128:256], (gx, oy, gz)),
    ]
    two = [send(src, dst, s2, r2, i, peer) for i, (src, dst, peer) in enumerate(ways)]

    fpad[...] = dot(fq[...].reshape(384, 768), cst[1280:2048, :]).astype(BF16)
    for g in range(2):
        total = None
        for c in range(9):
            term = dot_t(tfine[c], fpad[16 * c : 16 * c + 256, 256 * g : 256 * g + 512])
            total = term if total is None else total + term
        sfine[g] = total

    for copy in two:
        copy.wait_recv()
    fm[0:6, :, 0:256] = fm[0:6, :, 0:256] * keep_low
    fm[14:20, :, 0:256] = fm[14:20, :, 0:256] * keep_high
    cross_m = send(fm.at[:, :, 0:256], fm.at[:, :, 256:512], s2, r2, 5, (ox, gy, gz))

    @pl.loop(1, nz)
    def _(d):
        gather(d, lax.rem(gz + nz - d, nz)).wait_recv()

    high, low = split(gath[...].reshape(256, 512))
    fields = dot(ezr[0], high) + (dot(ezr[0], low) + dot(ezr[1], high))
    lane = lax.broadcasted_iota(jnp.int32, (16, 128), 1) // 32
    for j in range(4):
        tile = fields[:, 128 * j : 128 * j + 128]
        turns = [tile] + [pltpu.roll(tile, 32 * t, 1) for t in range(1, 4)]
        for i in range(4):
            m = 4 * j + i
            for t in range(2):
                block = None
                for s in range(4):
                    g = 4 * t + s
                    piece = turns[(s - i) % 4][16 * g : 16 * g + 16]
                    block = piece if block is None else jnp.where(lane == s, piece, block)
                amat[16 * m : 16 * m + 16, 128 * t : 128 * t + 128] = block
    high, low = split(amat[...])
    share = dot(high[0:128], wlo[0]) + dot(high[128:256], whi[0])
    share = share + (dot(low[0:128], wlo[0]) + dot(low[128:256], whi[0]))
    share = share + (dot(high[0:128], wlo[1]) + dot(high[128:256], whi[1]))
    share = jnp.swapaxes(share.reshape(8, 16, 512), 0, 1)
    for w in range(4):
        dmat[w] = share[0:10, :, 128 * w : 128 * w + 128]
    ways = [(oy + 2 * gx, (gx, oy, gz)), (oy + 2 * ox, (ox, oy, gz)), (gy + 2 * ox, (ox, gy, gz))]
    three = [send(dmat.at[w], rmat.at[i], s3, r3, i, peer) for i, (w, peer) in enumerate(ways)]

    cross_m.wait_recv()
    mpad[...] = dot(fm[...].reshape(320, 512), cst[2048:2560, :]).astype(BF16)
    for g in range(2):
        total = None
        for c in range(9):
            term = dot_t(mpad[16 * c : 16 * c + 192, 256 * g : 256 * g + 512], tmid[c])
            total = term if total is None else total + term
        smid[:, 256 * g : 256 * g + 256] = total

    def trimmed(mid):
        spot = lax.broadcasted_iota(jnp.int32, mid.shape, 0) - 2 + 8 * gz
        return jnp.where((spot >= 0) & (spot < 8 * nz), mid, 0.0)

    mid = trimmed(smid[...].reshape(12, 16, 512))
    fine = interleave(mid[2:10], widen(mid[1:12], 8)).reshape(256, 512)
    high, low = split(fine)
    back = cst[768:1152, 256:768]
    total = dot_t(back, high) + dot_t(back, low)
    total = total + sfine[...].reshape(16, 32, 256)[:, 0:24].reshape(384, 256)
    sfine_own = total

    for copy in three:
        copy.wait_recv()
    top = (dmat[variant] + rmat[2]) + (rmat[0] + rmat[1])
    mid = interleave(top[2:8], widen(top[1:10], 6))
    mid = trimmed(mid)
    fine = interleave(mid[2:10], widen(mid[1:12], 8))
    lower = lax.broadcasted_iota(jnp.int32, (16, 8, 128), 2) < 64
    fine = jnp.concatenate(
        [jnp.where(lower, fine, 0.0), jnp.where(lower, 0.0, fine)], axis=1
    ).reshape(256, 128)
    high, low = split(fine)
    up_high, up_low = cst[0:384, 384:512], cst[0:384, 512:640]
    result = dot_t(up_high, high) + (dot_t(up_high, low) + dot_t(up_low, high)) + sfine_own
    out_ref[...] = result.reshape(16, 24, 256)

    for copy in one + [cross_x] + two + [cross_m] + three:
        copy.wait_send()

    @pl.loop(1, nz)
    def _(d):
        gather(d, gz).wait_send()


def solution(mesh):
    whole, spread = constants()
    nz = mesh.shape["gz"]
    vmem = pl.BlockSpec(memory_space=pltpu.VMEM)
    dma = pltpu.SemaphoreType.DMA

    def per_device(charges, kernel_fine, kernel_mid, gauss_width, gauss_weight):
        return pl.pallas_call(
            kernel,
            out_shape=jax.ShapeDtypeStruct((16, 24, 256), F32),
            in_specs=[pl.BlockSpec(memory_space=pltpu.HBM)] * 7,
            out_specs=vmem,
            scratch_shapes=[
                pltpu.VMEM((16, 24, 256), BF16),
                pltpu.VMEM((9, 9, 9), BF16),
                pltpu.VMEM((9, 9, 9), BF16),
                pltpu.SMEM((GAUSS,), F32),
                pltpu.SMEM((GAUSS,), F32),
                pltpu.VMEM((32, 512), F32),
                pltpu.VMEM((16, 512), F32),
                pltpu.VMEM((ROWS_C, 768), BF16),
                pltpu.VMEM((24, 16, 768), BF16),
                pltpu.VMEM((16, 16, 128), BF16),
                pltpu.VMEM((24, 16, 256), BF16),
                pltpu.VMEM((384, 768), BF16),
                pltpu.VMEM((9, 256, 512), BF16),
                pltpu.VMEM((9, 256, 512), BF16),
                pltpu.VMEM((20, 16, 512), BF16),
                pltpu.VMEM((320, 768), BF16),
                pltpu.VMEM((nz, 8, 512), F32),
                pltpu.VMEM((2, 256, 256), F32),
                pltpu.VMEM((192, 512), F32),
                pltpu.VMEM((256, 256), F32),
                pltpu.VMEM((4, 10, 8, 128), F32),
                pltpu.VMEM((3, 10, 8, 128), F32),
                pltpu.VMEM((2, 128, 256), BF16),
                pltpu.VMEM((2, 256, 512), BF16),
                pltpu.VMEM((2, 256, 512), BF16),
                dma((8,)),
                dma((6,)), dma((6,)),
                dma((6,)), dma((6,)),
                dma((nz,)), dma((nz,)),
                dma((3,)), dma((3,)),
            ],
            compiler_params=pltpu.CompilerParams(
                collective_id=0, has_side_effects=True, vmem_limit_bytes=63 * 2**20
            ),
        )(
            charges, kernel_fine, kernel_mid, gauss_width, gauss_weight,
            jnp.asarray(whole), jnp.asarray(spread),
        )

    placed = (P("gx", "gy", "gz"), P(), P(), P(), P())
    return jax.shard_map(
        per_device, mesh=mesh, in_specs=placed, out_specs=P("gx", "gy", "gz"), check_vma=False
    )
```

```python
import jax
import jax.numpy as jnp
import numpy as np
import ml_dtypes
from jax import lax
from jax.experimental import pallas as pl
from jax.experimental.pallas import tpu as pltpu
from jax.sharding import PartitionSpec as P

M = 16
GAUSS = 8
MESH = pl.DeviceIdType.MESH
F32 = jnp.float32
BF16 = jnp.bfloat16


def weight(offset):
    return {0: 1.0, 1: 9 / 16, 3: -1 / 16}.get(abs(offset), 0.0)


def halo_list(side, size):
    if side == 0:
        return [size, size + 1, size + 2, size + 3, size + 5, None, None, None]
    return [-9, -7, -6, -5, -4, -3, -2, -1]


def extra_list(side, size):
    return [size + 1] if side == 0 else [-3, -1]


def cross(xs, ys):
    return [None if (x is None or y is None) else (x, y) for x in xs for y in ys]


def moved(coords, dx, dy):
    return [None if c is None else (c[0] + dx, c[1] + dy) for c in coords]


def padded(coords, size):
    return coords + [None] * (size - len(coords))


def picker(source, target):
    table = np.zeros((len(source), len(target)), np.float32)
    for j, c in enumerate(target):
        for i, other in enumerate(source):
            if c is not None and c == other:
                table[i, j] = 1.0
    return table


def weights_between(fine, coarse):
    table = np.zeros((len(fine), len(coarse)), np.float32)
    for i, f in enumerate(fine):
        if f is None:
            continue
        for j, c in enumerate(coarse):
            if c is not None:
                table[i, j] = weight(f[0] - 2 * c[0]) * weight(f[1] - 2 * c[1])
    return table


ROWS_A = 512
ROWS_C = 2560


def plane(gx, gy):
    yl = [24, 25, 26, 27] if gy == 0 else [-4, -3, -2, -1]
    xl = halo_list(gx, 16)
    own = cross(range(16), range(24))
    edge = cross(range(16), yl)
    fine = own + edge + edge + cross(xl, list(range(24)) + yl + [None] * 4)
    mid_own = cross(range(8), range(12))
    mid = padded(mid_own + cross(extra_list(gx, 8), range(12)), 128)
    return own, fine, mid_own, mid


def constants():
    whole = np.zeros((4, ROWS_C, 768), np.float32)
    spread = np.full((4, 32, 512), 1e30, np.float32)
    for gx in range(2):
        for gy in range(2):
            v = gx * 2 + gy
            own, fine, mid_own, mid = plane(gx, gy)
            out = whole[v]
            dy = 24 if gy == 0 else -24
            dx = 16 if gx == 0 else -16
            other_y = plane(gx, 1 - gy)[1]
            other_x = plane(1 - gx, gy)[1]
            out[0:384, 256:384] = picker(own, moved(other_y[384:512], 0, dy))
            out[0:512, 0:256] = picker(fine[:512], moved(other_x[512:768], dx, 0))
            xs = range(0, 7) if gx == 0 else range(-3, 4)
            ys = range(0, 9) if gy == 0 else range(-3, 6)
            window = padded(cross(xs, ys), 64)
            inside = cross(
                range(0, 10) if gx == 0 else range(-2, 8), range(0, 14) if gy == 0 else range(-2, 12)
            )
            up = weights_between(own, inside).astype(np.float64) @ weights_between(inside, window)
            up = np.concatenate([up, up], axis=1)
            high = up.astype(ml_dtypes.bfloat16).astype(np.float64)
            out[0:384, 384:512] = high
            out[0:384, 512:640] = up - high
            rz = np.zeros((256, 128), np.float32)
            for j in range(256):
                for i in range(128):
                    rz[j, i] = weight(j - 2 * i)
            empty = np.zeros((32, 8, 128), np.float32)
            rz = rz.reshape(32, 8, 128)
            out[0:512, 640:768] = np.stack([rz, empty], axis=1).reshape(512, 128)
            out[512:1024, 128:256] = np.stack([empty, rz], axis=1).reshape(512, 128)
            out[512:1280, 0:128] = weights_between(fine, mid)
            top = cross(range(4), list(range(8)) if gy == 0 else list(range(-1, 6)) + [None])
            out[512:640, 256:768] = np.tile(weights_between(mid, top), (1, 16))
            lanes = [c if c in set(inside) else None for c in cross(range(-2, 14), range(-2, 30))]
            out[768:1152, 256:768] = weights_between(own, lanes)
            out[1280:2048] = picker(fine, cross(range(-4, 20), range(-4, 28)))
            blocks = []
            for bx in (0, dx // 2):
                for by in (0, dy // 2):
                    blocks += padded(moved(mid_own, bx, by), 128)
            out[2048:2560] = picker(blocks, cross(range(-6, 18), range(-6, 26)))
            for i, c in enumerate(top):
                if c is None:
                    continue
                for wx in range(2):
                    for wy in range(2):
                        for xi in range(7):
                            for yi in range(9):
                                d = (4 * gx + c[0] - wx - xi) ** 2 + (6 * gy + c[1] - 3 * wy - yi) ** 2
                                lane = (wx * 2 + wy) * 128 + xi * 9 + yi
                                spread[v, i, lane] = d
                                spread[v, i, lane + 64] = d
    return whole.astype(ml_dtypes.bfloat16), spread


def dot(a, b):
    return lax.dot_general(a, b, (((1,), (0,)), ((), ())), preferred_element_type=F32)


def dot_t(a, b):
    return lax.dot_general(a, b, (((1,), (1,)), ((), ())), preferred_element_type=F32)


def split(a):
    high = a.astype(BF16)
    return high, (a - high.astype(F32)).astype(BF16)


def widen(a, count):
    near, far = 9.0 / 16.0, -1.0 / 16.0
    odd = near * (a[1 : count + 1] + a[2 : count + 2]) + far * (a[0:count] + a[3 : count + 3])
    return odd


def interleave(even, odd):
    both = jnp.concatenate([even[:, None], odd[:, None]], axis=1)
    return both.reshape((2 * even.shape[0],) + even.shape[1:])


def kernel(
    q_hbm, kf_hbm, km_hbm, gw_hbm, gg_hbm, cst_hbm, spread_hbm, out_ref,
    q_ref, kf_ref, km_ref, gw_ref, gg_ref, spread_ref, base, cst, fq, py, yb, yz, px, fpad, tfine, tmid, fm, mpad, gath, sfine, smid, amat, dmat, rmat, ezr, wlo, whi,
    cst_sem, s1, r1, s2, r2, sg, rg, s3, r3,
):
    gx, gy, gz = lax.axis_index("gx"), lax.axis_index("gy"), lax.axis_index("gz")
    nz = lax.axis_size("gz")
    ox, oy = 1 - gx, 1 - gy
    up, down = lax.rem(gz + 1, nz), lax.rem(gz + nz - 1, nz)
    variant = gx * 2 + gy

    first = pltpu.make_async_copy(
        cst_hbm.at[variant, pl.ds(0, ROWS_A)], cst.at[pl.ds(0, ROWS_A)], cst_sem.at[0]
    )
    rest = pltpu.make_async_copy(
        cst_hbm.at[variant, pl.ds(ROWS_A, ROWS_C - ROWS_A)],
        cst.at[pl.ds(ROWS_A, ROWS_C - ROWS_A)],
        cst_sem.at[1],
    )
    inputs = [
        pltpu.make_async_copy(src, dst, cst_sem.at[2 + i])
        for i, (src, dst) in enumerate(
            (
                (q_hbm, q_ref), (kf_hbm, kf_ref), (km_hbm, km_ref), (gw_hbm, gw_ref),
                (gg_hbm, gg_ref), (spread_hbm.at[variant], spread_ref),
            )
        )
    ]
    for copy in inputs[:2]:
        copy.start()
    first.start()
    for copy in inputs[2:]:
        copy.start()
    rest.start()

    barrier = pltpu.get_barrier_semaphore()
    for peer in ((ox, gy, gz), (gx, oy, gz), (ox, oy, gz), (gx, oy, up), (gx, oy, down)):
        pl.semaphore_signal(barrier, inc=1, device_id=peer, device_id_type=MESH)

    @pl.loop(1, nz)
    def _(d):
        pl.semaphore_signal(
            barrier, inc=1, device_id=(gx, gy, lax.rem(gz + d, nz)), device_id_type=MESH
        )

    inputs[0].wait()
    turned = q_ref[...].astype(F32).reshape(384, 256).T.astype(BF16)
    fq[4:20, :, 0:384] = turned.reshape(16, 16, 384)
    first.wait()
    edge = dot(turned, cst[0:384, 256:384]).reshape(16, 16, 128)
    low_half = lax.broadcasted_iota(jnp.int32, (8, 16, 128), 2) < 64
    py[...] = jnp.where(low_half, edge[0:8], edge[8:16]).astype(BF16)

    def build(k_ref, table):
        lane = lax.broadcasted_iota(jnp.int32, (9, 512), 1)
        row = lax.broadcasted_iota(jnp.int32, (9, 512), 0)
        total = jnp.zeros((9, 512), F32)
        for a in range(9):
            place = (lane == row + 32 * a).astype(F32).astype(BF16)
            total = total + lax.dot_general(
                k_ref[a], place, (((0,), (0,)), ((), ())), preferred_element_type=F32
            )
        base[0:9] = total

        @pl.loop(0, 9)
        def _(c):
            line = jnp.broadcast_to(base[pl.ds(c, 1)], (16, 512))
            strip = pltpu.roll(line, 0, 1, stride=1, stride_axis=0)
            for i in range(8):
                part = pltpu.roll(strip, 16 * i, 1).astype(BF16)
                table[c, 16 * i : 16 * i + 16, :] = part
                table[c, 128 + 16 * i : 144 + 16 * i, 0:128] = part[:, 384:512]
                table[c, 128 + 16 * i : 144 + 16 * i, 128:512] = part[:, 0:384]

    pl.semaphore_wait(barrier, nz - 1 + 5)

    def send(src, dst, sems, recvs, i, peer):
        copy = pltpu.make_async_remote_copy(
            src_ref=src, dst_ref=dst, send_sem=sems.at[i], recv_sem=recvs.at[i],
            device_id=peer, device_id_type=MESH,
        )
        copy.start()
        return copy

    ways = [
        (py.at[4:8], yz.at[0:4], (gx, oy, up)),
        (py.at[0:4], yz.at[4:8], (gx, oy, down)),
        (fq.at[16:20, :, 0:384], fq.at[0:4, :, 0:384], (gx, gy, up)),
        (fq.at[4:8, :, 0:384], fq.at[20:24, :, 0:384], (gx, gy, down)),
        (py, yb, (gx, oy, gz)),
    ]
    one = [send(src, dst, s1, r1, i, peer) for i, (src, dst, peer) in enumerate(ways)]

    for copy in inputs[1:]:
        copy.wait()
    build(kf_ref, tfine)
    build(km_ref, tmid)
    rest.wait()
    node = gz * 4 - 3 + lax.broadcasted_iota(jnp.int32, (16, 128), 0)
    gap = (node - lax.broadcasted_iota(jnp.int32, (16, 128), 1)).astype(F32)
    exists = (node >= 0) & (node < 4 * nz)
    half = lax.rem(lax.broadcasted_iota(jnp.int32, (32, 512), 1), 128) < 64
    parts = []
    for g in range(GAUSS):
        width = jnp.full((16, 128), gw_ref[g], F32)
        ratio = gap / width
        parts.append(jnp.where(exists, jnp.exp(-(ratio * ratio)) / jnp.sqrt(width), 0.0))
        width = jnp.full((32, 512), gw_ref[g], F32)
        both = jnp.exp(-(spread_ref[...] / (width * width))) * (gg_ref[g] / width)
        for table, keep in ((wlo, half), (whi, jnp.logical_not(half))):
            high, low = split(jnp.where(keep, both, 0.0))
            table[0, 32 * g : 32 * g + 32] = high
            table[1, 32 * g : 32 * g + 32] = low
    ez = jnp.concatenate(parts, axis=0)
    high, low = split(ez)
    low2 = (ez - high.astype(F32) - low.astype(F32)).astype(BF16)
    for h, rz in enumerate((cst[0:512, 640:768], cst[512:1024, 128:256])):
        first_half, second = split(dot_t(high, rz) + dot_t(low, rz) + dot_t(low2, rz))
        ezr[h, 0] = first_half
        ezr[h, 1] = second

    for copy in one:
        copy.wait_recv()
    keep_low = (gz > 0).astype(F32).astype(BF16)
    keep_high = (gz < nz - 1).astype(F32).astype(BF16)
    fq[0:4, :, 0:384] = fq[0:4, :, 0:384] * keep_low
    fq[20:24, :, 0:384] = fq[20:24, :, 0:384] * keep_high
    in_low = low_half.astype(F32).astype(BF16)
    in_high = jnp.logical_not(low_half).astype(F32).astype(BF16)
    fq[0:4, :, 384:512] = yz[0:4] * in_high[0:4] * keep_low
    fq[4:12, :, 384:512] = yb[...] * in_low
    fq[12:20, :, 384:512] = yb[...] * in_high
    fq[20:24, :, 384:512] = yz[4:8] * in_low[0:4] * keep_high
    known = fq[:, :, 0:512].reshape(384, 512)
    px[...] = dot(known, cst[0:512, 0:256]).astype(BF16).reshape(24, 16, 256)
    cross_x = send(px, fq.at[:, :, 512:768], s1, r1, 5, (ox, gy, gz))
    plane_mid = dot(known, cst[512:1024, 0:128])
    cross_x.wait_recv()
    plane_mid = plane_mid + dot(fq[:, :, 512:768].reshape(384, 256), cst[1024:1280, 0:128])
    rows = plane_mid.reshape(12, 2, 16, 128)
    even, odd = rows[:, 0], rows[:, 1]
    q_mid = (
        even[2:10]
        + (9.0 / 16.0) * (odd[1:9] + odd[2:10])
        + (-1.0 / 16.0) * (odd[0:8] + odd[3:11])
    ).astype(BF16)
    fm[6:14, :, 0:128] = q_mid
    tops = dot(q_mid.reshape(128, 128), cst[512:640, 256:768]).reshape(8, 16, 512)
    member = lax.broadcasted_iota(jnp.int32, (16, 512), 0)
    group = lax.broadcasted_iota(jnp.int32, (16, 512), 1) // 32
    tops = jnp.sum(jnp.where((member == group)[None], tops, 0.0), axis=1)
    sent, error = [], jnp.zeros((1, 512), F32)
    for z in range(8):
        value = tops[z : z + 1] + error
        sent.append(value.astype(BF16).astype(F32))
        error = value - sent[-1]
    sent = jnp.concatenate(sent, axis=0)
    gath[gz] = jnp.concatenate([sent[:, 0:256], sent[:, 256:512]], axis=0).astype(BF16)

    def gather(d, slot):
        return pltpu.make_async_remote_copy(
            src_ref=gath.at[slot], dst_ref=gath.at[slot], send_sem=sg.at[d], recv_sem=rg.at[slot],
            device_id=(gx, gy, lax.rem(gz + d, nz)), device_id_type=MESH,
        )

    @pl.loop(1, nz)
    def _(d):
        gather(d, gz).start()

    ways = [
        (fm.at[8:14, :, 0:128], fm.at[0:6, :, 128:256], (gx, oy, up)),
        (fm.at[6:12, :, 0:128], fm.at[14:20, :, 128:256], (gx, oy, down)),
        (fm.at[8:14, :, 0:128], fm.at[0:6, :, 0:128], (gx, gy, up)),
        (fm.at[6:12, :, 0:128], fm.at[14:20, :, 0:128], (gx, gy, down)),
        (fm.at[6:14, :, 0:128], fm.at[6:14, :, 128:256], (gx, oy, gz)),
    ]
    two = [send(src, dst, s2, r2, i, peer) for i, (src, dst, peer) in enumerate(ways)]

    fpad[...] = dot(fq[...].reshape(384, 768), cst[1280:2048, :]).astype(BF16)
    for g in range(2):
        total = None
        for c in range(9):
            term = dot_t(tfine[c], fpad[16 * c : 16 * c + 256, 256 * g : 256 * g + 512])
            total = term if total is None else total + term
        sfine[g] = total

    for copy in two:
        copy.wait_recv()
    fm[0:6, :, 0:256] = fm[0:6, :, 0:256] * keep_low
    fm[14:20, :, 0:256] = fm[14:20, :, 0:256] * keep_high
    cross_m = send(fm.at[:, :, 0:256], fm.at[:, :, 256:512], s2, r2, 5, (ox, gy, gz))

    @pl.loop(1, nz)
    def _(d):
        gather(d, lax.rem(gz + nz - d, nz)).wait_recv()

    got = gath[...].reshape(512, 256)
    fields = jnp.concatenate([dot(ezr[h, 0], got) + dot(ezr[h, 1], got) for h in range(2)], axis=1)
    lane = lax.broadcasted_iota(jnp.int32, (16, 128), 1) // 32
    for j in range(4):
        tile = fields[:, 128 * j : 128 * j + 128]
        turns = [tile] + [pltpu.roll(tile, 32 * t, 1) for t in range(1, 4)]
        for i in range(4):
            m = 4 * j + i
            for t in range(2):
                block = None
                for s in range(4):
                    g = 4 * t + s
                    piece = turns[(s - i) % 4][16 * g : 16 * g + 16]
                    block = piece if block is None else jnp.where(lane == s, piece, block)
                amat[16 * m : 16 * m + 16, 128 * t : 128 * t + 128] = block
    high, low = split(amat[...])
    share = dot(high[0:128], wlo[0]) + dot(high[128:256], whi[0])
    share = share + (dot(low[0:128], wlo[0]) + dot(low[128:256], whi[0]))
    share = share + (dot(high[0:128], wlo[1]) + dot(high[128:256], whi[1]))
    share = jnp.swapaxes(share.reshape(8, 16, 512), 0, 1)
    for w in range(4):
        dmat[w] = share[0:10, :, 128 * w : 128 * w + 128]
    ways = [(oy + 2 * gx, (gx, oy, gz)), (oy + 2 * ox, (ox, oy, gz)), (gy + 2 * ox, (ox, gy, gz))]
    three = [send(dmat.at[w], rmat.at[i], s3, r3, i, peer) for i, (w, peer) in enumerate(ways)]

    cross_m.wait_recv()
    mpad[...] = dot(fm[...].reshape(320, 512), cst[2048:2560, :]).astype(BF16)
    for g in range(2):
        total = None
        for c in range(9):
            term = dot_t(mpad[16 * c : 16 * c + 192, 256 * g : 256 * g + 512], tmid[c])
            total = term if total is None else total + term
        smid[:, 256 * g : 256 * g + 256] = total

    def trimmed(mid):
        spot = lax.broadcasted_iota(jnp.int32, mid.shape, 0) - 2 + 8 * gz
        return jnp.where((spot >= 0) & (spot < 8 * nz), mid, 0.0)

    mid = trimmed(smid[...].reshape(12, 16, 512))
    fine = interleave(mid[2:10], widen(mid[1:12], 8)).reshape(256, 512)
    high, low = split(fine)
    back = cst[768:1152, 256:768]
    total = dot_t(back, high) + dot_t(back, low)
    total = total + sfine[...].reshape(16, 32, 256)[:, 0:24].reshape(384, 256)
    sfine_own = total

    for copy in three:
        copy.wait_recv()
    top = (dmat[variant] + rmat[2]) + (rmat[0] + rmat[1])
    mid = interleave(top[2:8], widen(top[1:10], 6))
    mid = trimmed(mid)
    fine = interleave(mid[2:10], widen(mid[1:12], 8))
    lower = lax.broadcasted_iota(jnp.int32, (16, 8, 128), 2) < 64
    fine = jnp.concatenate(
        [jnp.where(lower, fine, 0.0), jnp.where(lower, 0.0, fine)], axis=1
    ).reshape(256, 128)
    high, low = split(fine)
    up_high, up_low = cst[0:384, 384:512], cst[0:384, 512:640]
    result = dot_t(up_high, high) + (dot_t(up_high, low) + dot_t(up_low, high)) + sfine_own
    out_ref[...] = result.reshape(16, 24, 256)

    for copy in one + [cross_x] + two + [cross_m] + three:
        copy.wait_send()

    @pl.loop(1, nz)
    def _(d):
        gather(d, gz).wait_send()


def solution(mesh):
    whole, spread = constants()
    nz = mesh.shape["gz"]
    vmem = pl.BlockSpec(memory_space=pltpu.VMEM)
    dma = pltpu.SemaphoreType.DMA

    def per_device(charges, kernel_fine, kernel_mid, gauss_width, gauss_weight):
        return pl.pallas_call(
            kernel,
            out_shape=jax.ShapeDtypeStruct((16, 24, 256), F32),
            in_specs=[pl.BlockSpec(memory_space=pltpu.HBM)] * 7,
            out_specs=vmem,
            scratch_shapes=[
                pltpu.VMEM((16, 24, 256), BF16),
                pltpu.VMEM((9, 9, 9), BF16),
                pltpu.VMEM((9, 9, 9), BF16),
                pltpu.SMEM((GAUSS,), F32),
                pltpu.SMEM((GAUSS,), F32),
                pltpu.VMEM((32, 512), F32),
                pltpu.VMEM((16, 512), F32),
                pltpu.VMEM((ROWS_C, 768), BF16),
                pltpu.VMEM((24, 16, 768), BF16),
                pltpu.VMEM((8, 16, 128), BF16),
                pltpu.VMEM((8, 16, 128), BF16),
                pltpu.VMEM((8, 16, 128), BF16),
                pltpu.VMEM((24, 16, 256), BF16),
                pltpu.VMEM((384, 768), BF16),
                pltpu.VMEM((9, 256, 512), BF16),
                pltpu.VMEM((9, 256, 512), BF16),
                pltpu.VMEM((20, 16, 512), BF16),
                pltpu.VMEM((320, 768), BF16),
                pltpu.VMEM((nz, 16, 256), BF16),
                pltpu.VMEM((2, 256, 256), F32),
                pltpu.VMEM((192, 512), F32),
                pltpu.VMEM((256, 256), F32),
                pltpu.VMEM((4, 10, 8, 128), F32),
                pltpu.VMEM((3, 10, 8, 128), F32),
                pltpu.VMEM((2, 2, 128, 512), BF16),
                pltpu.VMEM((2, 256, 512), BF16),
                pltpu.VMEM((2, 256, 512), BF16),
                dma((8,)),
                dma((6,)), dma((6,)),
                dma((6,)), dma((6,)),
                dma((nz,)), dma((nz,)),
                dma((3,)), dma((3,)),
            ],
            compiler_params=pltpu.CompilerParams(
                collective_id=0, has_side_effects=True, vmem_limit_bytes=63 * 2**20
            ),
        )(
            charges, kernel_fine, kernel_mid, gauss_width, gauss_weight,
            jnp.asarray(whole), jnp.asarray(spread),
        )

    placed = (P("gx", "gy", "gz"), P(), P(), P(), P())
    return jax.shard_map(
        per_device, mesh=mesh, in_specs=placed, out_specs=P("gx", "gy", "gz"), check_vma=False
    )
```

```python
import jax
import jax.numpy as jnp
import numpy as np
import ml_dtypes
from jax import lax
from jax.experimental import pallas as pl
from jax.experimental.pallas import tpu as pltpu
from jax.sharding import PartitionSpec as P

M = 16
GAUSS = 8
MESH = pl.DeviceIdType.MESH
F32 = jnp.float32
BF16 = jnp.bfloat16


def weight(offset):
    return {0: 1.0, 1: 9 / 16, 3: -1 / 16}.get(abs(offset), 0.0)


def halo_list(side, size):
    if side == 0:
        return [size, size + 1, size + 2, size + 3, size + 5, None, None, None]
    return [-9, -7, -6, -5, -4, -3, -2, -1]


def extra_list(side, size):
    return [size + 1] if side == 0 else [-3, -1]


def cross(xs, ys):
    return [None if (x is None or y is None) else (x, y) for x in xs for y in ys]


def moved(coords, dx, dy):
    return [None if c is None else (c[0] + dx, c[1] + dy) for c in coords]


def padded(coords, size):
    return coords + [None] * (size - len(coords))


def picker(source, target):
    table = np.zeros((len(source), len(target)), np.float32)
    for j, c in enumerate(target):
        for i, other in enumerate(source):
            if c is not None and c == other:
                table[i, j] = 1.0
    return table


def weights_between(fine, coarse):
    table = np.zeros((len(fine), len(coarse)), np.float32)
    for i, f in enumerate(fine):
        if f is None:
            continue
        for j, c in enumerate(coarse):
            if c is not None:
                table[i, j] = weight(f[0] - 2 * c[0]) * weight(f[1] - 2 * c[1])
    return table


ROWS_A = 512
ROWS_C = 2560


def plane(gx, gy):
    yl = [24, 25, 26, 27] if gy == 0 else [-4, -3, -2, -1]
    xl = halo_list(gx, 16)
    own = cross(range(16), range(24))
    edge = cross(range(16), yl)
    fine = own + edge + edge + cross(xl, list(range(24)) + yl + [None] * 4)
    mid_own = cross(range(8), range(12))
    mid = padded(mid_own + cross(extra_list(gx, 8), range(12)), 128)
    return own, fine, mid_own, mid


def constants():
    whole = np.zeros((4, ROWS_C, 768), np.float32)
    spread = np.full((4, 32, 512), 1e30, np.float32)
    for gx in range(2):
        for gy in range(2):
            v = gx * 2 + gy
            own, fine, mid_own, mid = plane(gx, gy)
            out = whole[v]
            dy = 24 if gy == 0 else -24
            dx = 16 if gx == 0 else -16
            other_y = plane(gx, 1 - gy)[1]
            other_x = plane(1 - gx, gy)[1]
            out[0:384, 256:384] = picker(own, moved(other_y[384:512], 0, dy))
            out[0:512, 0:256] = picker(fine[:512], moved(other_x[512:768], dx, 0))
            xs = range(0, 7) if gx == 0 else range(-3, 4)
            ys = range(0, 9) if gy == 0 else range(-3, 6)
            window = padded(cross(xs, ys), 64)
            inside = cross(
                range(0, 10) if gx == 0 else range(-2, 8), range(0, 14) if gy == 0 else range(-2, 12)
            )
            up = weights_between(own, inside).astype(np.float64) @ weights_between(inside, window)
            up = np.concatenate([up, up], axis=1)
            high = up.astype(ml_dtypes.bfloat16).astype(np.float64)
            out[0:384, 384:512] = high
            out[0:384, 512:640] = up - high
            rz = np.zeros((256, 128), np.float32)
            for j in range(256):
                for i in range(128):
                    rz[j, i] = weight(j - 2 * i)
            empty = np.zeros((32, 8, 128), np.float32)
            rz = rz.reshape(32, 8, 128)
            out[0:512, 640:768] = np.stack([rz, empty], axis=1).reshape(512, 128)
            out[512:1024, 128:256] = np.stack([empty, rz], axis=1).reshape(512, 128)
            out[512:1280, 0:128] = weights_between(fine, mid)
            top = cross(range(4), list(range(8)) if gy == 0 else list(range(-1, 6)) + [None])
            out[512:640, 256:768] = np.tile(weights_between(mid, top), (1, 16))
            lanes = [c if c in set(inside) else None for c in cross(range(-2, 14), range(-2, 30))]
            out[768:1152, 256:768] = weights_between(own, lanes)
            out[1280:2048] = picker(fine, cross(range(-4, 20), range(-4, 28)))
            blocks = []
            for bx in (0, dx // 2):
                for by in (0, dy // 2):
                    blocks += padded(moved(mid_own, bx, by), 128)
            out[2048:2560] = picker(blocks, cross(range(-6, 18), range(-6, 26)))
            for i, c in enumerate(top):
                if c is None:
                    continue
                for wx in range(2):
                    for wy in range(2):
                        for xi in range(7):
                            for yi in range(9):
                                d = (4 * gx + c[0] - wx - xi) ** 2 + (6 * gy + c[1] - 3 * wy - yi) ** 2
                                lane = (wx * 2 + wy) * 128 + xi * 9 + yi
                                spread[v, i, lane] = d
                                spread[v, i, lane + 64] = d
    return whole.astype(ml_dtypes.bfloat16), spread


def dot(a, b):
    return lax.dot_general(a, b, (((1,), (0,)), ((), ())), preferred_element_type=F32)


def dot_t(a, b):
    return lax.dot_general(a, b, (((1,), (1,)), ((), ())), preferred_element_type=F32)


def split(a):
    high = a.astype(BF16)
    return high, (a - high.astype(F32)).astype(BF16)


def widen(a, count):
    near, far = 9.0 / 16.0, -1.0 / 16.0
    odd = near * (a[1 : count + 1] + a[2 : count + 2]) + far * (a[0:count] + a[3 : count + 3])
    return odd


def interleave(even, odd):
    both = jnp.concatenate([even[:, None], odd[:, None]], axis=1)
    return both.reshape((2 * even.shape[0],) + even.shape[1:])


def kernel(
    q_hbm, kf_hbm, km_hbm, gw_hbm, gg_hbm, cst_hbm, spread_hbm, out_ref,
    q_ref, kf_ref, km_ref, gw_ref, gg_ref, spread_ref, base, cst, fq, py, yb, yz, px, fpad, tfine, tmid, fm, mpad, gath, sfine, smid, amat, dmat, rmat, ezr, wlo, whi,
    cst_sem, s1, r1, s2, r2, sg, rg, s3, r3,
):
    gx, gy, gz = lax.axis_index("gx"), lax.axis_index("gy"), lax.axis_index("gz")
    nz = lax.axis_size("gz")
    ox, oy = 1 - gx, 1 - gy
    up, down = lax.rem(gz + 1, nz), lax.rem(gz + nz - 1, nz)
    variant = gx * 2 + gy

    first = pltpu.make_async_copy(
        cst_hbm.at[variant, pl.ds(0, ROWS_A)], cst.at[pl.ds(0, ROWS_A)], cst_sem.at[0]
    )
    rest = pltpu.make_async_copy(
        cst_hbm.at[variant, pl.ds(ROWS_A, ROWS_C - ROWS_A)],
        cst.at[pl.ds(ROWS_A, ROWS_C - ROWS_A)],
        cst_sem.at[1],
    )
    inputs = [
        pltpu.make_async_copy(src, dst, cst_sem.at[2 + i])
        for i, (src, dst) in enumerate(
            (
                (q_hbm, q_ref), (kf_hbm, kf_ref), (km_hbm, km_ref), (gw_hbm, gw_ref),
                (gg_hbm, gg_ref), (spread_hbm.at[variant], spread_ref),
            )
        )
    ]
    for copy in inputs[:2]:
        copy.start()
    first.start()
    for copy in inputs[2:]:
        copy.start()
    rest.start()

    far_first = sorted(
        range(1, nz), key=lambda d: -min(d // 8, 4 - d // 8) - min(d // 2 % 4, 4 - d // 2 % 4)
    )
    barrier = pltpu.get_barrier_semaphore()
    for peer in ((ox, gy, gz), (gx, oy, gz), (ox, oy, gz), (gx, oy, up), (gx, oy, down)):
        pl.semaphore_signal(barrier, inc=1, device_id=peer, device_id_type=MESH)

    for d in far_first:
        pl.semaphore_signal(
            barrier, inc=1, device_id=(gx, gy, lax.rem(gz + d, nz)), device_id_type=MESH
        )

    inputs[0].wait()
    turned = q_ref[...].astype(F32).reshape(384, 256).T.astype(BF16)
    fq[4:20, :, 0:384] = turned.reshape(16, 16, 384)
    first.wait()
    edge = dot(turned, cst[0:384, 256:384]).reshape(16, 16, 128)
    low_half = lax.broadcasted_iota(jnp.int32, (8, 16, 128), 2) < 64
    py[...] = jnp.where(low_half, edge[0:8], edge[8:16]).astype(BF16)

    def build(k_ref, table):
        lane = lax.broadcasted_iota(jnp.int32, (9, 512), 1)
        row = lax.broadcasted_iota(jnp.int32, (9, 512), 0)
        total = jnp.zeros((9, 512), F32)
        for a in range(9):
            place = (lane == row + 32 * a).astype(F32).astype(BF16)
            total = total + lax.dot_general(
                k_ref[a], place, (((0,), (0,)), ((), ())), preferred_element_type=F32
            )
        base[0:9] = total

        @pl.loop(0, 9)
        def _(c):
            line = jnp.broadcast_to(base[pl.ds(c, 1)], (16, 512))
            strip = pltpu.roll(line, 0, 1, stride=1, stride_axis=0)
            for i in range(8):
                part = pltpu.roll(strip, 16 * i, 1).astype(BF16)
                table[c, 16 * i : 16 * i + 16, :] = part
                table[c, 128 + 16 * i : 144 + 16 * i, 0:128] = part[:, 384:512]
                table[c, 128 + 16 * i : 144 + 16 * i, 128:512] = part[:, 0:384]

    pl.semaphore_wait(barrier, nz - 1 + 5)

    def send(src, dst, sems, recvs, i, peer):
        copy = pltpu.make_async_remote_copy(
            src_ref=src, dst_ref=dst, send_sem=sems.at[i], recv_sem=recvs.at[i],
            device_id=peer, device_id_type=MESH,
        )
        copy.start()
        return copy

    ways = [
        (py.at[4:8], yz.at[0:4], (gx, oy, up)),
        (py.at[0:4], yz.at[4:8], (gx, oy, down)),
        (fq.at[16:20, :, 0:384], fq.at[0:4, :, 0:384], (gx, gy, up)),
        (fq.at[4:8, :, 0:384], fq.at[20:24, :, 0:384], (gx, gy, down)),
        (py, yb, (gx, oy, gz)),
    ]
    one = [send(src, dst, s1, r1, i, peer) for i, (src, dst, peer) in enumerate(ways)]

    for copy in inputs[1:]:
        copy.wait()
    build(kf_ref, tfine)
    build(km_ref, tmid)
    rest.wait()
    node = gz * 4 - 3 + lax.broadcasted_iota(jnp.int32, (16, 128), 0)
    gap = (node - lax.broadcasted_iota(jnp.int32, (16, 128), 1)).astype(F32)
    exists = (node >= 0) & (node < 4 * nz)
    half = lax.rem(lax.broadcasted_iota(jnp.int32, (32, 512), 1), 128) < 64
    parts = []
    for g in range(GAUSS):
        width = jnp.full((16, 128), gw_ref[g], F32)
        ratio = gap / width
        parts.append(jnp.where(exists, jnp.exp(-(ratio * ratio)) / jnp.sqrt(width), 0.0))
        width = jnp.full((32, 512), gw_ref[g], F32)
        both = jnp.exp(-(spread_ref[...] / (width * width))) * (gg_ref[g] / width)
        for table, keep in ((wlo, half), (whi, jnp.logical_not(half))):
            high, low = split(jnp.where(keep, both, 0.0))
            table[0, 32 * g : 32 * g + 32] = high
            table[1, 32 * g : 32 * g + 32] = low
    ez = jnp.concatenate(parts, axis=0)
    high, low = split(ez)
    low2 = (ez - high.astype(F32) - low.astype(F32)).astype(BF16)
    for h, rz in enumerate((cst[0:512, 640:768], cst[512:1024, 128:256])):
        first_half, second = split(dot_t(high, rz) + dot_t(low, rz) + dot_t(low2, rz))
        ezr[h, 0] = first_half
        ezr[h, 1] = second

    for copy in one:
        copy.wait_recv()
    keep_low = (gz > 0).astype(F32).astype(BF16)
    keep_high = (gz < nz - 1).astype(F32).astype(BF16)
    fq[0:4, :, 0:384] = fq[0:4, :, 0:384] * keep_low
    fq[20:24, :, 0:384] = fq[20:24, :, 0:384] * keep_high
    in_low = low_half.astype(F32).astype(BF16)
    in_high = jnp.logical_not(low_half).astype(F32).astype(BF16)
    fq[0:4, :, 384:512] = yz[0:4] * in_high[0:4] * keep_low
    fq[4:12, :, 384:512] = yb[...] * in_low
    fq[12:20, :, 384:512] = yb[...] * in_high
    fq[20:24, :, 384:512] = yz[4:8] * in_low[0:4] * keep_high
    known = fq[:, :, 0:512].reshape(384, 512)
    px[...] = dot(known, cst[0:512, 0:256]).astype(BF16).reshape(24, 16, 256)
    cross_x = send(px, fq.at[:, :, 512:768], s1, r1, 5, (ox, gy, gz))
    plane_mid = dot(known, cst[512:1024, 0:128])
    cross_x.wait_recv()
    plane_mid = plane_mid + dot(fq[:, :, 512:768].reshape(384, 256), cst[1024:1280, 0:128])
    rows = plane_mid.reshape(12, 2, 16, 128)
    even, odd = rows[:, 0], rows[:, 1]
    q_mid = (
        even[2:10]
        + (9.0 / 16.0) * (odd[1:9] + odd[2:10])
        + (-1.0 / 16.0) * (odd[0:8] + odd[3:11])
    ).astype(BF16)
    fm[6:14, :, 0:128] = q_mid
    tops = dot(q_mid.reshape(128, 128), cst[512:640, 256:768]).reshape(8, 16, 512)
    member = lax.broadcasted_iota(jnp.int32, (16, 512), 0)
    group = lax.broadcasted_iota(jnp.int32, (16, 512), 1) // 32
    tops = jnp.sum(jnp.where((member == group)[None], tops, 0.0), axis=1)
    sent, error = [], jnp.zeros((1, 512), F32)
    for z in range(8):
        value = tops[z : z + 1] + error
        sent.append(value.astype(BF16).astype(F32))
        error = value - sent[-1]
    sent = jnp.concatenate(sent, axis=0)
    gath[gz] = jnp.concatenate([sent[:, 0:256], sent[:, 256:512]], axis=0).astype(BF16)

    def gather(d, slot):
        return pltpu.make_async_remote_copy(
            src_ref=gath.at[slot], dst_ref=gath.at[slot], send_sem=sg.at[d], recv_sem=rg.at[slot],
            device_id=(gx, gy, lax.rem(gz + d, nz)), device_id_type=MESH,
        )

    @pl.loop(1, nz)
    def _(d):
        gather(d, gz).start()

    ways = [
        (fm.at[8:14, :, 0:128], fm.at[0:6, :, 128:256], (gx, oy, up)),
        (fm.at[6:12, :, 0:128], fm.at[14:20, :, 128:256], (gx, oy, down)),
        (fm.at[8:14, :, 0:128], fm.at[0:6, :, 0:128], (gx, gy, up)),
        (fm.at[6:12, :, 0:128], fm.at[14:20, :, 0:128], (gx, gy, down)),
        (fm.at[6:14, :, 0:128], fm.at[6:14, :, 128:256], (gx, oy, gz)),
    ]
    two = [send(src, dst, s2, r2, i, peer) for i, (src, dst, peer) in enumerate(ways)]

    fpad[...] = dot(fq[...].reshape(384, 768), cst[1280:2048, :]).astype(BF16)
    for g in range(2):
        total = None
        for c in range(9):
            term = dot_t(tfine[c], fpad[16 * c : 16 * c + 256, 256 * g : 256 * g + 512])
            total = term if total is None else total + term
        sfine[g] = total

    for d in far_first:
        gather(d, lax.rem(gz + nz - d, nz)).wait_recv()

    got = gath[...].reshape(512, 256)
    fields = jnp.concatenate([dot(ezr[h, 0], got) + dot(ezr[h, 1], got) for h in range(2)], axis=1)
    lane = lax.broadcasted_iota(jnp.int32, (16, 128), 1) // 32
    for j in range(4):
        tile = fields[:, 128 * j : 128 * j + 128]
        turns = [tile] + [pltpu.roll(tile, 32 * t, 1) for t in range(1, 4)]
        for i in range(4):
            m = 4 * j + i
            for t in range(2):
                block = None
                for s in range(4):
                    g = 4 * t + s
                    piece = turns[(s - i) % 4][16 * g : 16 * g + 16]
                    block = piece if block is None else jnp.where(lane == s, piece, block)
                amat[16 * m : 16 * m + 16, 128 * t : 128 * t + 128] = block
    high, low = split(amat[...])
    share = dot(high[0:128], wlo[0]) + dot(high[128:256], whi[0])
    share = share + (dot(low[0:128], wlo[0]) + dot(low[128:256], whi[0]))
    share = share + (dot(high[0:128], wlo[1]) + dot(high[128:256], whi[1]))
    share = jnp.swapaxes(share.reshape(8, 16, 512), 0, 1)
    for w in range(4):
        dmat[w] = share[0:10, :, 128 * w : 128 * w + 128]
    ways = [(oy + 2 * gx, (gx, oy, gz)), (oy + 2 * ox, (ox, oy, gz)), (gy + 2 * ox, (ox, gy, gz))]
    three = [send(dmat.at[w], rmat.at[i], s3, r3, i, peer) for i, (w, peer) in enumerate(ways)]

    for copy in two:
        copy.wait_recv()
    fm[0:6, :, 0:256] = fm[0:6, :, 0:256] * keep_low
    fm[14:20, :, 0:256] = fm[14:20, :, 0:256] * keep_high
    cross_m = send(fm.at[:, :, 0:256], fm.at[:, :, 256:512], s2, r2, 5, (ox, gy, gz))

    cross_m.wait_recv()
    mpad[...] = dot(fm[...].reshape(320, 512), cst[2048:2560, :]).astype(BF16)
    for g in range(2):
        total = None
        for c in range(9):
            term = dot_t(mpad[16 * c : 16 * c + 192, 256 * g : 256 * g + 512], tmid[c])
            total = term if total is None else total + term
        smid[:, 256 * g : 256 * g + 256] = total

    def trimmed(mid):
        spot = lax.broadcasted_iota(jnp.int32, mid.shape, 0) - 2 + 8 * gz
        return jnp.where((spot >= 0) & (spot < 8 * nz), mid, 0.0)

    mid = trimmed(smid[...].reshape(12, 16, 512))
    fine = interleave(mid[2:10], widen(mid[1:12], 8)).reshape(256, 512)
    high, low = split(fine)
    back = cst[768:1152, 256:768]
    total = dot_t(back, high) + dot_t(back, low)
    total = total + sfine[...].reshape(16, 32, 256)[:, 0:24].reshape(384, 256)
    sfine_own = total

    for copy in one + [cross_x] + two:
        copy.wait_send()

    @pl.loop(1, nz)
    def _(d):
        gather(d, gz).wait_send()

    for copy in three:
        copy.wait_recv()
    top = (dmat[variant] + rmat[2]) + (rmat[0] + rmat[1])
    mid = interleave(top[2:8], widen(top[1:10], 6))
    mid = trimmed(mid)
    fine = interleave(mid[2:10], widen(mid[1:12], 8))
    lower = lax.broadcasted_iota(jnp.int32, (16, 8, 128), 2) < 64
    fine = jnp.concatenate(
        [jnp.where(lower, fine, 0.0), jnp.where(lower, 0.0, fine)], axis=1
    ).reshape(256, 128)
    high, low = split(fine)
    up_high, up_low = cst[0:384, 384:512], cst[0:384, 512:640]
    result = dot_t(up_high, high) + (dot_t(up_high, low) + dot_t(up_low, high)) + sfine_own
    out_ref[...] = result.reshape(16, 24, 256)

    for copy in [cross_m] + three:
        copy.wait_send()


def solution(mesh):
    whole, spread = constants()
    nz = mesh.shape["gz"]
    vmem = pl.BlockSpec(memory_space=pltpu.VMEM)
    dma = pltpu.SemaphoreType.DMA

    def per_device(charges, kernel_fine, kernel_mid, gauss_width, gauss_weight):
        return pl.pallas_call(
            kernel,
            out_shape=jax.ShapeDtypeStruct((16, 24, 256), F32),
            in_specs=[pl.BlockSpec(memory_space=pltpu.HBM)] * 7,
            out_specs=vmem,
            scratch_shapes=[
                pltpu.VMEM((16, 24, 256), BF16),
                pltpu.VMEM((9, 9, 9), BF16),
                pltpu.VMEM((9, 9, 9), BF16),
                pltpu.SMEM((GAUSS,), F32),
                pltpu.SMEM((GAUSS,), F32),
                pltpu.VMEM((32, 512), F32),
                pltpu.VMEM((16, 512), F32),
                pltpu.VMEM((ROWS_C, 768), BF16),
                pltpu.VMEM((24, 16, 768), BF16),
                pltpu.VMEM((8, 16, 128), BF16),
                pltpu.VMEM((8, 16, 128), BF16),
                pltpu.VMEM((8, 16, 128), BF16),
                pltpu.VMEM((24, 16, 256), BF16),
                pltpu.VMEM((384, 768), BF16),
                pltpu.VMEM((9, 256, 512), BF16),
                pltpu.VMEM((9, 256, 512), BF16),
                pltpu.VMEM((20, 16, 512), BF16),
                pltpu.VMEM((320, 768), BF16),
                pltpu.VMEM((nz, 16, 256), BF16),
                pltpu.VMEM((2, 256, 256), F32),
                pltpu.VMEM((192, 512), F32),
                pltpu.VMEM((256, 256), F32),
                pltpu.VMEM((4, 10, 8, 128), F32),
                pltpu.VMEM((3, 10, 8, 128), F32),
                pltpu.VMEM((2, 2, 128, 512), BF16),
                pltpu.VMEM((2, 256, 512), BF16),
                pltpu.VMEM((2, 256, 512), BF16),
                dma((8,)),
                dma((6,)), dma((6,)),
                dma((6,)), dma((6,)),
                dma((nz,)), dma((nz,)),
                dma((3,)), dma((3,)),
            ],
            compiler_params=pltpu.CompilerParams(
                collective_id=0, has_side_effects=True, vmem_limit_bytes=63 * 2**20
            ),
        )(
            charges, kernel_fine, kernel_mid, gauss_width, gauss_weight,
            jnp.asarray(whole), jnp.asarray(spread),
        )

    placed = (P("gx", "gy", "gz"), P(), P(), P(), P())
    return jax.shard_map(
        per_device, mesh=mesh, in_specs=placed, out_specs=P("gx", "gy", "gz"), check_vma=False
    )
```

```python
import jax
import jax.numpy as jnp
import numpy as np
import ml_dtypes
from jax import lax
from jax.experimental import pallas as pl
from jax.experimental.pallas import tpu as pltpu
from jax.sharding import PartitionSpec as P

M = 16
GAUSS = 8
MESH = pl.DeviceIdType.MESH
F32 = jnp.float32
BF16 = jnp.bfloat16


def weight(offset):
    return {0: 1.0, 1: 9 / 16, 3: -1 / 16}.get(abs(offset), 0.0)


def halo_list(side, size):
    if side == 0:
        return [size, size + 1, size + 2, size + 3, size + 5, None, None, None]
    return [-9, -7, -6, -5, -4, -3, -2, -1]


def extra_list(side, size):
    return [size + 1] if side == 0 else [-3, -1]


def cross(xs, ys):
    return [None if (x is None or y is None) else (x, y) for x in xs for y in ys]


def moved(coords, dx, dy):
    return [None if c is None else (c[0] + dx, c[1] + dy) for c in coords]


def padded(coords, size):
    return coords + [None] * (size - len(coords))


def picker(source, target):
    table = np.zeros((len(source), len(target)), np.float32)
    for j, c in enumerate(target):
        for i, other in enumerate(source):
            if c is not None and c == other:
                table[i, j] = 1.0
    return table


def weights_between(fine, coarse):
    table = np.zeros((len(fine), len(coarse)), np.float32)
    for i, f in enumerate(fine):
        if f is None:
            continue
        for j, c in enumerate(coarse):
            if c is not None:
                table[i, j] = weight(f[0] - 2 * c[0]) * weight(f[1] - 2 * c[1])
    return table


ROWS_A = 512
ROWS_C = 2560


def plane(gx, gy):
    yl = [24, 25, 26, 27] if gy == 0 else [-4, -3, -2, -1]
    xl = halo_list(gx, 16)
    own = cross(range(16), range(24))
    edge = cross(range(16), yl)
    fine = own + edge + edge + cross(xl, list(range(24)) + yl + [None] * 4)
    mid_own = cross(range(8), range(12))
    mid = padded(mid_own + cross(extra_list(gx, 8), range(12)), 128)
    return own, fine, mid_own, mid


def constants():
    whole = np.zeros((4, ROWS_C, 768), np.float32)
    spread = np.full((4, 32, 512), 1e30, np.float32)
    for gx in range(2):
        for gy in range(2):
            v = gx * 2 + gy
            own, fine, mid_own, mid = plane(gx, gy)
            out = whole[v]
            dy = 24 if gy == 0 else -24
            dx = 16 if gx == 0 else -16
            other_y = plane(gx, 1 - gy)[1]
            other_x = plane(1 - gx, gy)[1]
            out[0:384, 256:384] = picker(own, moved(other_y[384:512], 0, dy))
            out[0:512, 0:256] = picker(fine[:512], moved(other_x[512:768], dx, 0))
            xs = range(0, 7) if gx == 0 else range(-3, 4)
            ys = range(0, 9) if gy == 0 else range(-3, 6)
            window = padded(cross(xs, ys), 64)
            inside = cross(
                range(0, 10) if gx == 0 else range(-2, 8), range(0, 14) if gy == 0 else range(-2, 12)
            )
            up = weights_between(own, inside).astype(np.float64) @ weights_between(inside, window)
            up = np.concatenate([up, up], axis=1)
            high = up.astype(ml_dtypes.bfloat16).astype(np.float64)
            out[0:384, 384:512] = high
            out[0:384, 512:640] = up - high
            rz = np.zeros((256, 128), np.float32)
            for j in range(256):
                for i in range(128):
                    rz[j, i] = weight(j - 2 * i)
            empty = np.zeros((32, 8, 128), np.float32)
            rz = rz.reshape(32, 8, 128)
            out[0:512, 640:768] = np.stack([rz, empty], axis=1).reshape(512, 128)
            out[512:1024, 128:256] = np.stack([empty, rz], axis=1).reshape(512, 128)
            out[512:1280, 0:128] = weights_between(fine, mid)
            top = cross(range(4), list(range(8)) if gy == 0 else list(range(-1, 6)) + [None])
            out[512:640, 256:768] = np.tile(weights_between(mid, top), (1, 16))
            lanes = [c if c in set(inside) else None for c in cross(range(-2, 14), range(-2, 30))]
            out[768:1152, 256:768] = weights_between(own, lanes)
            out[1280:2048] = picker(fine, cross(range(-4, 20), range(-4, 28)))
            blocks = []
            for bx in (0, dx // 2):
                for by in (0, dy // 2):
                    blocks += padded(moved(mid_own, bx, by), 128)
            out[2048:2560] = picker(blocks, cross(range(-6, 18), range(-6, 26)))
            for i, c in enumerate(top):
                if c is None:
                    continue
                for wx in range(2):
                    for wy in range(2):
                        for xi in range(7):
                            for yi in range(9):
                                d = (4 * gx + c[0] - wx - xi) ** 2 + (6 * gy + c[1] - 3 * wy - yi) ** 2
                                lane = (wx * 2 + wy) * 128 + xi * 9 + yi
                                spread[v, i, lane] = d
                                spread[v, i, lane + 64] = d
    return whole.astype(ml_dtypes.bfloat16), spread


def dot(a, b):
    return lax.dot_general(a, b, (((1,), (0,)), ((), ())), preferred_element_type=F32)


def dot_t(a, b):
    return lax.dot_general(a, b, (((1,), (1,)), ((), ())), preferred_element_type=F32)


def split(a):
    high = a.astype(BF16)
    return high, (a - high.astype(F32)).astype(BF16)


def widen(a, count):
    near, far = 9.0 / 16.0, -1.0 / 16.0
    odd = near * (a[1 : count + 1] + a[2 : count + 2]) + far * (a[0:count] + a[3 : count + 3])
    return odd


def interleave(even, odd):
    both = jnp.concatenate([even[:, None], odd[:, None]], axis=1)
    return both.reshape((2 * even.shape[0],) + even.shape[1:])


def kernel(
    q_hbm, kf_hbm, km_hbm, gw_hbm, gg_hbm, cst_hbm, spread_hbm, out_ref,
    q_ref, kf_ref, km_ref, gw_ref, gg_ref, spread_ref, base, cst, fq, py, yb, yz, px, fpad, tfine, tmid, fm, mpad, gath, sfine, smid, amat, dmat, rmat, ezr, wlo, whi,
    cst_sem, s1, r1, s2, r2, sg, rg, s3, r3,
):
    gx, gy, gz = lax.axis_index("gx"), lax.axis_index("gy"), lax.axis_index("gz")
    nz = lax.axis_size("gz")
    ox, oy = 1 - gx, 1 - gy
    up, down = lax.rem(gz + 1, nz), lax.rem(gz + nz - 1, nz)
    variant = gx * 2 + gy

    first = pltpu.make_async_copy(
        cst_hbm.at[variant, pl.ds(0, ROWS_A)], cst.at[pl.ds(0, ROWS_A)], cst_sem.at[0]
    )
    rest = pltpu.make_async_copy(
        cst_hbm.at[variant, pl.ds(ROWS_A, ROWS_C - ROWS_A)],
        cst.at[pl.ds(ROWS_A, ROWS_C - ROWS_A)],
        cst_sem.at[1],
    )
    inputs = [
        pltpu.make_async_copy(src, dst, cst_sem.at[2 + i])
        for i, (src, dst) in enumerate(
            (
                (q_hbm, q_ref), (kf_hbm, kf_ref), (km_hbm, km_ref), (gw_hbm, gw_ref),
                (gg_hbm, gg_ref), (spread_hbm.at[variant], spread_ref),
            )
        )
    ]
    for copy in inputs[:2]:
        copy.start()
    first.start()
    for copy in inputs[2:]:
        copy.start()
    rest.start()

    far_first = sorted(
        range(1, nz), key=lambda d: -min(d // 8, 4 - d // 8) - min(d // 2 % 4, 4 - d // 2 % 4)
    )
    barrier = pltpu.get_barrier_semaphore()
    for peer in ((ox, gy, gz), (gx, oy, gz), (ox, oy, gz), (gx, oy, up), (gx, oy, down)):
        pl.semaphore_signal(barrier, inc=1, device_id=peer, device_id_type=MESH)

    for d in far_first:
        pl.semaphore_signal(
            barrier, inc=1, device_id=(gx, gy, lax.rem(gz + d, nz)), device_id_type=MESH
        )

    inputs[0].wait()
    turned = q_ref[...].astype(F32).reshape(384, 256).T.astype(BF16)
    fq[4:20, :, 0:384] = turned.reshape(16, 16, 384)
    first.wait()
    edge = dot(turned, cst[0:384, 256:384]).reshape(16, 16, 128)
    low_half = lax.broadcasted_iota(jnp.int32, (8, 16, 128), 2) < 64
    py[...] = jnp.where(low_half, edge[0:8], edge[8:16]).astype(BF16)

    def build(k_ref, table):
        lane = lax.broadcasted_iota(jnp.int32, (9, 512), 1)
        row = lax.broadcasted_iota(jnp.int32, (9, 512), 0)
        total = jnp.zeros((9, 512), F32)
        for a in range(9):
            place = (lane == row + 32 * a).astype(F32).astype(BF16)
            total = total + lax.dot_general(
                k_ref[a], place, (((0,), (0,)), ((), ())), preferred_element_type=F32
            )
        base[0:9] = total

        @pl.loop(0, 9)
        def _(c):
            line = jnp.broadcast_to(base[pl.ds(c, 1)], (16, 512))
            strip = pltpu.roll(line, 0, 1, stride=1, stride_axis=0)
            for i in range(8):
                part = pltpu.roll(strip, 16 * i, 1).astype(BF16)
                table[c, 16 * i : 16 * i + 16, :] = part
                table[c, 128 + 16 * i : 144 + 16 * i, 0:128] = part[:, 384:512]
                table[c, 128 + 16 * i : 144 + 16 * i, 128:512] = part[:, 0:384]

    pl.semaphore_wait(barrier, nz - 1 + 5)

    def send(src, dst, sems, recvs, i, peer):
        copy = pltpu.make_async_remote_copy(
            src_ref=src, dst_ref=dst, send_sem=sems.at[i], recv_sem=recvs.at[i],
            device_id=peer, device_id_type=MESH,
        )
        copy.start()
        return copy

    ways = [
        (py.at[5:8], yz.at[1:4], (gx, oy, up)),
        (py.at[0:2], yz.at[4:6], (gx, oy, down)),
        (fq.at[17:20, :, 0:384], fq.at[1:4, :, 0:384], (gx, gy, up)),
        (fq.at[4:6, :, 0:384], fq.at[20:22, :, 0:384], (gx, gy, down)),
        (py, yb, (gx, oy, gz)),
        (py.at[4:5], yz.at[0:1], (gx, oy, up)),
        (py.at[2:4], yz.at[6:8], (gx, oy, down)),
        (fq.at[16:17, :, 0:384], fq.at[0:1, :, 0:384], (gx, gy, up)),
        (fq.at[6:8, :, 0:384], fq.at[22:24, :, 0:384], (gx, gy, down)),
    ]
    one = [send(src, dst, s1, r1, i, peer) for i, (src, dst, peer) in enumerate(ways)]

    for copy in inputs[1:]:
        copy.wait()
    build(kf_ref, tfine)
    build(km_ref, tmid)
    rest.wait()
    node = gz * 4 - 3 + lax.broadcasted_iota(jnp.int32, (16, 128), 0)
    gap = (node - lax.broadcasted_iota(jnp.int32, (16, 128), 1)).astype(F32)
    exists = (node >= 0) & (node < 4 * nz)
    half = lax.rem(lax.broadcasted_iota(jnp.int32, (32, 512), 1), 128) < 64
    parts = []
    for g in range(GAUSS):
        width = jnp.full((16, 128), gw_ref[g], F32)
        ratio = gap / width
        parts.append(jnp.where(exists, jnp.exp(-(ratio * ratio)) / jnp.sqrt(width), 0.0))
        width = jnp.full((32, 512), gw_ref[g], F32)
        both = jnp.exp(-(spread_ref[...] / (width * width))) * (gg_ref[g] / width)
        for table, keep in ((wlo, half), (whi, jnp.logical_not(half))):
            high, low = split(jnp.where(keep, both, 0.0))
            table[0, 32 * g : 32 * g + 32] = high
            table[1, 32 * g : 32 * g + 32] = low
    ez = jnp.concatenate(parts, axis=0)
    high, low = split(ez)
    low2 = (ez - high.astype(F32) - low.astype(F32)).astype(BF16)
    for h, rz in enumerate((cst[0:512, 640:768], cst[512:1024, 128:256])):
        first_half, second = split(dot_t(high, rz) + dot_t(low, rz) + dot_t(low2, rz))
        ezr[h, 0] = first_half
        ezr[h, 1] = second

    for copy in one[:5]:
        copy.wait_recv()
    keep_low = (gz > 0).astype(F32).astype(BF16)
    keep_high = (gz < nz - 1).astype(F32).astype(BF16)
    in_low = low_half.astype(F32).astype(BF16)
    in_high = jnp.logical_not(low_half).astype(F32).astype(BF16)
    fq[1:4, :, 0:384] = fq[1:4, :, 0:384] * keep_low
    fq[20:22, :, 0:384] = fq[20:22, :, 0:384] * keep_high
    fq[1:4, :, 384:512] = yz[1:4] * in_high[0:3] * keep_low
    fq[4:12, :, 384:512] = yb[...] * in_low
    fq[12:20, :, 384:512] = yb[...] * in_high
    fq[20:22, :, 384:512] = yz[4:6] * in_low[0:2] * keep_high
    known = fq[1:22, :, 0:512].reshape(336, 512)
    px[1:22] = dot(known, cst[0:512, 0:256]).astype(BF16).reshape(21, 16, 256)
    cross_x = [send(px.at[1:22], fq.at[1:22, :, 512:768], s1, r1, 9, (ox, gy, gz))]
    plane_mid = dot(known, cst[512:1024, 0:128])
    cross_x[0].wait_recv()
    plane_mid = plane_mid + dot(fq[1:22, :, 512:768].reshape(336, 256), cst[1024:1280, 0:128])
    rows = plane_mid.reshape(21, 16, 128)
    rows = jnp.concatenate([rows, rows[0:1]], axis=0).reshape(11, 2, 16, 128)
    odd, even = rows[:, 0], rows[:, 1]
    q_mid = (
        even[1:9]
        + (9.0 / 16.0) * (odd[1:9] + odd[2:10])
        + (-1.0 / 16.0) * (odd[0:8] + odd[3:11])
    ).astype(BF16)
    fm[6:14, :, 0:128] = q_mid
    tops = dot(q_mid.reshape(128, 128), cst[512:640, 256:768]).reshape(8, 16, 512)
    member = lax.broadcasted_iota(jnp.int32, (16, 512), 0)
    group = lax.broadcasted_iota(jnp.int32, (16, 512), 1) // 32
    tops = jnp.sum(jnp.where((member == group)[None], tops, 0.0), axis=1)
    sent, error = [], jnp.zeros((1, 512), F32)
    for z in range(8):
        value = tops[z : z + 1] + error
        sent.append(value.astype(BF16).astype(F32))
        error = value - sent[-1]
    sent = jnp.concatenate(sent, axis=0)
    gath[gz] = jnp.concatenate([sent[:, 0:256], sent[:, 256:512]], axis=0).astype(BF16)

    def gather(d, slot):
        return pltpu.make_async_remote_copy(
            src_ref=gath.at[slot], dst_ref=gath.at[slot], send_sem=sg.at[d], recv_sem=rg.at[slot],
            device_id=(gx, gy, lax.rem(gz + d, nz)), device_id_type=MESH,
        )

    @pl.loop(1, nz)
    def _(d):
        gather(d, gz).start()

    ways = [
        (fm.at[8:14, :, 0:128], fm.at[0:6, :, 128:256], (gx, oy, up)),
        (fm.at[6:12, :, 0:128], fm.at[14:20, :, 128:256], (gx, oy, down)),
        (fm.at[8:14, :, 0:128], fm.at[0:6, :, 0:128], (gx, gy, up)),
        (fm.at[6:12, :, 0:128], fm.at[14:20, :, 0:128], (gx, gy, down)),
        (fm.at[6:14, :, 0:128], fm.at[6:14, :, 128:256], (gx, oy, gz)),
    ]
    two = [send(src, dst, s2, r2, i, peer) for i, (src, dst, peer) in enumerate(ways)]

    for copy in one[5:]:
        copy.wait_recv()
    for where, other, keep in (
        (slice(0, 1), yz[0:1] * in_high[0:1], keep_low), (slice(22, 24), yz[6:8] * in_low[0:2], keep_high)
    ):
        count = where.stop - where.start
        fq[where, :, 0:384] = fq[where, :, 0:384] * keep
        fq[where, :, 384:512] = other * keep
        px[where] = dot(fq[where, :, 0:512].reshape(16 * count, 512), cst[0:512, 0:256]).astype(
            BF16
        ).reshape(count, 16, 256)
    cross_x += [
        send(px.at[0:1], fq.at[0:1, :, 512:768], s1, r1, 10, (ox, gy, gz)),
        send(px.at[22:24], fq.at[22:24, :, 512:768], s1, r1, 11, (ox, gy, gz)),
    ]
    for copy in cross_x[1:]:
        copy.wait_recv()
    fpad[...] = dot(fq[...].reshape(384, 768), cst[1280:2048, :]).astype(BF16)
    for g in range(2):
        total = None
        for c in range(9):
            term = dot_t(tfine[c], fpad[16 * c : 16 * c + 256, 256 * g : 256 * g + 512])
            total = term if total is None else total + term
        sfine[g] = total

    for d in far_first:
        gather(d, lax.rem(gz + nz - d, nz)).wait_recv()

    got = gath[...].reshape(512, 256)
    fields = jnp.concatenate([dot(ezr[h, 0], got) + dot(ezr[h, 1], got) for h in range(2)], axis=1)
    lane = lax.broadcasted_iota(jnp.int32, (16, 128), 1) // 32
    for j in range(4):
        tile = fields[:, 128 * j : 128 * j + 128]
        turns = [tile] + [pltpu.roll(tile, 32 * t, 1) for t in range(1, 4)]
        for i in range(4):
            m = 4 * j + i
            for t in range(2):
                block = None
                for s in range(4):
                    g = 4 * t + s
                    piece = turns[(s - i) % 4][16 * g : 16 * g + 16]
                    block = piece if block is None else jnp.where(lane == s, piece, block)
                amat[16 * m : 16 * m + 16, 128 * t : 128 * t + 128] = block
    high, low = split(amat[...])
    share = dot(high[0:128], wlo[0]) + dot(high[128:256], whi[0])
    share = share + (dot(low[0:128], wlo[0]) + dot(low[128:256], whi[0]))
    share = share + (dot(high[0:128], wlo[1]) + dot(high[128:256], whi[1]))
    share = jnp.swapaxes(share.reshape(8, 16, 512), 0, 1)
    for w in range(4):
        dmat[w] = share[0:10, :, 128 * w : 128 * w + 128]
    ways = [(oy + 2 * gx, (gx, oy, gz)), (oy + 2 * ox, (ox, oy, gz)), (gy + 2 * ox, (ox, gy, gz))]
    three = [send(dmat.at[w], rmat.at[i], s3, r3, i, peer) for i, (w, peer) in enumerate(ways)]

    for copy in two:
        copy.wait_recv()
    fm[0:6, :, 0:256] = fm[0:6, :, 0:256] * keep_low
    fm[14:20, :, 0:256] = fm[14:20, :, 0:256] * keep_high
    cross_m = send(fm.at[:, :, 0:256], fm.at[:, :, 256:512], s2, r2, 5, (ox, gy, gz))

    cross_m.wait_recv()
    mpad[...] = dot(fm[...].reshape(320, 512), cst[2048:2560, :]).astype(BF16)
    for g in range(2):
        total = None
        for c in range(9):
            term = dot_t(mpad[16 * c : 16 * c + 192, 256 * g : 256 * g + 512], tmid[c])
            total = term if total is None else total + term
        smid[:, 256 * g : 256 * g + 256] = total

    def trimmed(mid):
        spot = lax.broadcasted_iota(jnp.int32, mid.shape, 0) - 2 + 8 * gz
        return jnp.where((spot >= 0) & (spot < 8 * nz), mid, 0.0)

    mid = trimmed(smid[...].reshape(12, 16, 512))
    fine = interleave(mid[2:10], widen(mid[1:12], 8)).reshape(256, 512)
    high, low = split(fine)
    back = cst[768:1152, 256:768]
    total = dot_t(back, high) + dot_t(back, low)
    total = total + sfine[...].reshape(16, 32, 256)[:, 0:24].reshape(384, 256)
    sfine_own = total

    for copy in one + cross_x + two:
        copy.wait_send()

    @pl.loop(1, nz)
    def _(d):
        gather(d, gz).wait_send()

    for copy in three:
        copy.wait_recv()
    top = (dmat[variant] + rmat[2]) + (rmat[0] + rmat[1])
    mid = interleave(top[2:8], widen(top[1:10], 6))
    mid = trimmed(mid)
    fine = interleave(mid[2:10], widen(mid[1:12], 8))
    lower = lax.broadcasted_iota(jnp.int32, (16, 8, 128), 2) < 64
    fine = jnp.concatenate(
        [jnp.where(lower, fine, 0.0), jnp.where(lower, 0.0, fine)], axis=1
    ).reshape(256, 128)
    high, low = split(fine)
    up_high, up_low = cst[0:384, 384:512], cst[0:384, 512:640]
    result = dot_t(up_high, high) + (dot_t(up_high, low) + dot_t(up_low, high)) + sfine_own
    out_ref[...] = result.reshape(16, 24, 256)

    for copy in [cross_m] + three:
        copy.wait_send()


def solution(mesh):
    whole, spread = constants()
    nz = mesh.shape["gz"]
    vmem = pl.BlockSpec(memory_space=pltpu.VMEM)
    dma = pltpu.SemaphoreType.DMA

    def per_device(charges, kernel_fine, kernel_mid, gauss_width, gauss_weight):
        return pl.pallas_call(
            kernel,
            out_shape=jax.ShapeDtypeStruct((16, 24, 256), F32),
            in_specs=[pl.BlockSpec(memory_space=pltpu.HBM)] * 7,
            out_specs=vmem,
            scratch_shapes=[
                pltpu.VMEM((16, 24, 256), BF16),
                pltpu.VMEM((9, 9, 9), BF16),
                pltpu.VMEM((9, 9, 9), BF16),
                pltpu.SMEM((GAUSS,), F32),
                pltpu.SMEM((GAUSS,), F32),
                pltpu.VMEM((32, 512), F32),
                pltpu.VMEM((16, 512), F32),
                pltpu.VMEM((ROWS_C, 768), BF16),
                pltpu.VMEM((24, 16, 768), BF16),
                pltpu.VMEM((8, 16, 128), BF16),
                pltpu.VMEM((8, 16, 128), BF16),
                pltpu.VMEM((8, 16, 128), BF16),
                pltpu.VMEM((24, 16, 256), BF16),
                pltpu.VMEM((384, 768), BF16),
                pltpu.VMEM((9, 256, 512), BF16),
                pltpu.VMEM((9, 256, 512), BF16),
                pltpu.VMEM((20, 16, 512), BF16),
                pltpu.VMEM((320, 768), BF16),
                pltpu.VMEM((nz, 16, 256), BF16),
                pltpu.VMEM((2, 256, 256), F32),
                pltpu.VMEM((192, 512), F32),
                pltpu.VMEM((256, 256), F32),
                pltpu.VMEM((4, 10, 8, 128), F32),
                pltpu.VMEM((3, 10, 8, 128), F32),
                pltpu.VMEM((2, 2, 128, 512), BF16),
                pltpu.VMEM((2, 256, 512), BF16),
                pltpu.VMEM((2, 256, 512), BF16),
                dma((8,)),
                dma((12,)), dma((12,)),
                dma((6,)), dma((6,)),
                dma((nz,)), dma((nz,)),
                dma((3,)), dma((3,)),
            ],
            compiler_params=pltpu.CompilerParams(
                collective_id=0, has_side_effects=True, vmem_limit_bytes=63 * 2**20
            ),
        )(
            charges, kernel_fine, kernel_mid, gauss_width, gauss_weight,
            jnp.asarray(whole), jnp.asarray(spread),
        )

    placed = (P("gx", "gy", "gz"), P(), P(), P(), P())
    return jax.shard_map(
        per_device, mesh=mesh, in_specs=placed, out_specs=P("gx", "gy", "gz"), check_vma=False
    )
```

```python
import jax
import jax.numpy as jnp
import numpy as np
import ml_dtypes
from jax import lax
from jax.experimental import pallas as pl
from jax.experimental.pallas import tpu as pltpu
from jax.sharding import PartitionSpec as P

M = 16
GAUSS = 8
MESH = pl.DeviceIdType.MESH
F32 = jnp.float32
BF16 = jnp.bfloat16


def weight(offset):
    return {0: 1.0, 1: 9 / 16, 3: -1 / 16}.get(abs(offset), 0.0)


def halo_list(side, size):
    if side == 0:
        return [size, size + 1, size + 2, size + 3, size + 5, None, None, None]
    return [-9, -7, -6, -5, -4, -3, -2, -1]


def extra_list(side, size):
    return [size + 1] if side == 0 else [-3, -1]


def cross(xs, ys):
    return [None if (x is None or y is None) else (x, y) for x in xs for y in ys]


def moved(coords, dx, dy):
    return [None if c is None else (c[0] + dx, c[1] + dy) for c in coords]


def padded(coords, size):
    return coords + [None] * (size - len(coords))


def picker(source, target):
    table = np.zeros((len(source), len(target)), np.float32)
    for j, c in enumerate(target):
        for i, other in enumerate(source):
            if c is not None and c == other:
                table[i, j] = 1.0
    return table


def weights_between(fine, coarse):
    table = np.zeros((len(fine), len(coarse)), np.float32)
    for i, f in enumerate(fine):
        if f is None:
            continue
        for j, c in enumerate(coarse):
            if c is not None:
                table[i, j] = weight(f[0] - 2 * c[0]) * weight(f[1] - 2 * c[1])
    return table


ROWS_A = 512
ROWS_C = 2560


def plane(gx, gy):
    yl = [24, 25, 26, 27] if gy == 0 else [-4, -3, -2, -1]
    xl = halo_list(gx, 16)
    own = cross(range(16), range(24))
    edge = cross(range(16), yl)
    fine = own + edge + edge + cross(xl, list(range(24)) + yl + [None] * 4)
    mid_own = cross(range(8), range(12))
    mid = padded(mid_own + cross(extra_list(gx, 8), range(12)), 128)
    return own, fine, mid_own, mid


def constants():
    whole = np.zeros((4, ROWS_C, 768), np.float32)
    spread = np.full((4, 32, 512), 1e30, np.float32)
    for gx in range(2):
        for gy in range(2):
            v = gx * 2 + gy
            own, fine, mid_own, mid = plane(gx, gy)
            out = whole[v]
            dy = 24 if gy == 0 else -24
            dx = 16 if gx == 0 else -16
            other_y = plane(gx, 1 - gy)[1]
            other_x = plane(1 - gx, gy)[1]
            out[0:384, 256:384] = picker(own, moved(other_y[384:512], 0, dy))
            out[0:512, 0:256] = picker(fine[:512], moved(other_x[512:768], dx, 0))
            xs = range(0, 7) if gx == 0 else range(-3, 4)
            ys = range(0, 9) if gy == 0 else range(-3, 6)
            window = padded(cross(xs, ys), 64)
            inside = cross(
                range(0, 10) if gx == 0 else range(-2, 8), range(0, 14) if gy == 0 else range(-2, 12)
            )
            up = weights_between(own, inside).astype(np.float64) @ weights_between(inside, window)
            up = np.concatenate([up, up], axis=1)
            high = up.astype(ml_dtypes.bfloat16).astype(np.float64)
            out[0:384, 384:512] = high
            out[0:384, 512:640] = up - high
            rz = np.zeros((256, 128), np.float32)
            for j in range(256):
                for i in range(128):
                    rz[j, i] = weight(j - 2 * i)
            empty = np.zeros((32, 8, 128), np.float32)
            rz = rz.reshape(32, 8, 128)
            out[0:512, 640:768] = np.stack([rz, empty], axis=1).reshape(512, 128)
            out[512:1024, 128:256] = np.stack([empty, rz], axis=1).reshape(512, 128)
            out[512:1280, 0:128] = weights_between(fine, mid)
            top = cross(range(4), list(range(8)) if gy == 0 else list(range(-1, 6)) + [None])
            out[512:640, 256:768] = np.tile(weights_between(mid, top), (1, 16))
            lanes = [c if c in set(inside) else None for c in cross(range(-2, 14), range(-2, 30))]
            out[768:1152, 256:768] = weights_between(own, lanes)
            out[1280:2048] = picker(fine, cross(range(-4, 20), range(-4, 28)))
            blocks = []
            for bx in (0, dx // 2):
                for by in (0, dy // 2):
                    blocks += padded(moved(mid_own, bx, by), 128)
            out[2048:2560] = picker(blocks, cross(range(-6, 18), range(-6, 26)))
            for i, c in enumerate(top):
                if c is None:
                    continue
                for wx in range(2):
                    for wy in range(2):
                        for xi in range(7):
                            for yi in range(9):
                                d = (4 * gx + c[0] - wx - xi) ** 2 + (6 * gy + c[1] - 3 * wy - yi) ** 2
                                lane = (wx * 2 + wy) * 128 + xi * 9 + yi
                                spread[v, i, lane] = d
                                spread[v, i, lane + 64] = d
    return whole.astype(ml_dtypes.bfloat16), spread


def dot(a, b):
    return lax.dot_general(a, b, (((1,), (0,)), ((), ())), preferred_element_type=F32)


def dot_t(a, b):
    return lax.dot_general(a, b, (((1,), (1,)), ((), ())), preferred_element_type=F32)


def split(a):
    high = a.astype(BF16)
    return high, (a - high.astype(F32)).astype(BF16)


def widen(a, count):
    near, far = 9.0 / 16.0, -1.0 / 16.0
    odd = near * (a[1 : count + 1] + a[2 : count + 2]) + far * (a[0:count] + a[3 : count + 3])
    return odd


def interleave(even, odd):
    both = jnp.concatenate([even[:, None], odd[:, None]], axis=1)
    return both.reshape((2 * even.shape[0],) + even.shape[1:])


def kernel(
    q_hbm, kf_hbm, km_hbm, gw_hbm, gg_hbm, cst_hbm, spread_hbm, out_ref,
    q_ref, kf_ref, km_ref, gw_ref, gg_ref, spread_ref, base, cst, fq, py, yb, yz, px, fpad, tfine, tmid, fm, mpad, gath, sfine, smid, amat, dmat, rmat, ezr, wlo, whi,
    cst_sem, s1, r1, s2, r2, sg, rg, s3, r3,
):
    gx, gy, gz = lax.axis_index("gx"), lax.axis_index("gy"), lax.axis_index("gz")
    nz = lax.axis_size("gz")
    ox, oy = 1 - gx, 1 - gy
    up, down = lax.rem(gz + 1, nz), lax.rem(gz + nz - 1, nz)
    variant = gx * 2 + gy

    first = pltpu.make_async_copy(
        cst_hbm.at[variant, pl.ds(0, ROWS_A)], cst.at[pl.ds(0, ROWS_A)], cst_sem.at[0]
    )
    rest = pltpu.make_async_copy(
        cst_hbm.at[variant, pl.ds(ROWS_A, ROWS_C - ROWS_A)],
        cst.at[pl.ds(ROWS_A, ROWS_C - ROWS_A)],
        cst_sem.at[1],
    )
    inputs = [
        pltpu.make_async_copy(src, dst, cst_sem.at[2 + i])
        for i, (src, dst) in enumerate(
            (
                (q_hbm, q_ref), (kf_hbm, kf_ref), (km_hbm, km_ref), (gw_hbm, gw_ref),
                (gg_hbm, gg_ref), (spread_hbm.at[variant], spread_ref),
            )
        )
    ]
    for copy in inputs[:2]:
        copy.start()
    first.start()
    for copy in inputs[2:]:
        copy.start()
    rest.start()

    far_first = sorted(
        range(1, nz), key=lambda d: -min(d // 8, 4 - d // 8) - min(d // 2 % 4, 4 - d // 2 % 4)
    )
    barrier = pltpu.get_barrier_semaphore()
    for peer in ((ox, gy, gz), (gx, oy, gz), (ox, oy, gz), (gx, oy, up), (gx, oy, down)):
        pl.semaphore_signal(barrier, inc=1, device_id=peer, device_id_type=MESH)

    for d in far_first:
        pl.semaphore_signal(
            barrier, inc=1, device_id=(gx, gy, lax.rem(gz + d, nz)), device_id_type=MESH
        )

    inputs[0].wait()
    turned = q_ref[...].astype(F32).reshape(384, 256).T.astype(BF16)
    fq[4:20, :, 0:384] = turned.reshape(16, 16, 384)
    first.wait()
    edge = dot(turned, cst[0:384, 256:384]).reshape(16, 16, 128)
    low_half = lax.broadcasted_iota(jnp.int32, (8, 16, 128), 2) < 64
    py[...] = jnp.where(low_half, edge[0:8], edge[8:16]).astype(BF16)

    def build(k_ref, table):
        lane = lax.broadcasted_iota(jnp.int32, (9, 512), 1)
        row = lax.broadcasted_iota(jnp.int32, (9, 512), 0)
        total = jnp.zeros((9, 512), F32)
        for a in range(9):
            place = (lane == row + 32 * a).astype(F32).astype(BF16)
            total = total + lax.dot_general(
                k_ref[a], place, (((0,), (0,)), ((), ())), preferred_element_type=F32
            )
        base[0:9] = total

        @pl.loop(0, 9)
        def _(c):
            line = jnp.broadcast_to(base[pl.ds(c, 1)], (16, 512))
            strip = pltpu.roll(line, 0, 1, stride=1, stride_axis=0)
            for i in range(8):
                part = pltpu.roll(strip, 16 * i, 1).astype(BF16)
                table[c, 16 * i : 16 * i + 16, :] = part
                table[c, 128 + 16 * i : 144 + 16 * i, 0:128] = part[:, 384:512]
                table[c, 128 + 16 * i : 144 + 16 * i, 128:512] = part[:, 0:384]

    pl.semaphore_wait(barrier, nz - 1 + 5)

    def send(src, dst, sems, recvs, i, peer):
        copy = pltpu.make_async_remote_copy(
            src_ref=src, dst_ref=dst, send_sem=sems.at[i], recv_sem=recvs.at[i],
            device_id=peer, device_id_type=MESH,
        )
        copy.start()
        return copy

    ways = [
        (py.at[5:8], yz.at[1:4], (gx, oy, up)),
        (py.at[0:2], yz.at[4:6], (gx, oy, down)),
        (fq.at[17:20, :, 0:384], fq.at[1:4, :, 0:384], (gx, gy, up)),
        (fq.at[4:6, :, 0:384], fq.at[20:22, :, 0:384], (gx, gy, down)),
        (py, yb, (gx, oy, gz)),
        (py.at[4:5], yz.at[0:1], (gx, oy, up)),
        (py.at[2:4], yz.at[6:8], (gx, oy, down)),
        (fq.at[16:17, :, 0:384], fq.at[0:1, :, 0:384], (gx, gy, up)),
        (fq.at[6:8, :, 0:384], fq.at[22:24, :, 0:384], (gx, gy, down)),
    ]
    one = [send(src, dst, s1, r1, i, peer) for i, (src, dst, peer) in enumerate(ways)]

    for copy in inputs[1:]:
        copy.wait()
    build(kf_ref, tfine)
    build(km_ref, tmid)
    rest.wait()
    node = gz * 4 - 3 + lax.broadcasted_iota(jnp.int32, (16, 128), 0)
    gap = (node - lax.broadcasted_iota(jnp.int32, (16, 128), 1)).astype(F32)
    exists = (node >= 0) & (node < 4 * nz)
    half = lax.rem(lax.broadcasted_iota(jnp.int32, (32, 512), 1), 128) < 64
    parts = []
    for g in range(GAUSS):
        width = jnp.full((16, 128), gw_ref[g], F32)
        ratio = gap / width
        parts.append(jnp.where(exists, jnp.exp(-(ratio * ratio)) / jnp.sqrt(width), 0.0))
        width = jnp.full((32, 512), gw_ref[g], F32)
        both = jnp.exp(-(spread_ref[...] / (width * width))) * (gg_ref[g] / width)
        for table, keep in ((wlo, half), (whi, jnp.logical_not(half))):
            high, low = split(jnp.where(keep, both, 0.0))
            table[0, 32 * g : 32 * g + 32] = high
            table[1, 32 * g : 32 * g + 32] = low
    ez = jnp.concatenate(parts, axis=0)
    high, low = split(ez)
    low2 = (ez - high.astype(F32) - low.astype(F32)).astype(BF16)
    for h, rz in enumerate((cst[0:512, 640:768], cst[512:1024, 128:256])):
        first_half, second = split(dot_t(high, rz) + dot_t(low, rz) + dot_t(low2, rz))
        ezr[h, 0] = first_half
        ezr[h, 1] = second

    for copy in one[:5]:
        copy.wait_recv()
    keep_low = (gz > 0).astype(F32).astype(BF16)
    keep_high = (gz < nz - 1).astype(F32).astype(BF16)
    in_low = low_half.astype(F32).astype(BF16)
    in_high = jnp.logical_not(low_half).astype(F32).astype(BF16)
    fq[1:4, :, 0:384] = fq[1:4, :, 0:384] * keep_low
    fq[20:22, :, 0:384] = fq[20:22, :, 0:384] * keep_high
    fq[1:4, :, 384:512] = yz[1:4] * in_high[0:3] * keep_low
    fq[4:12, :, 384:512] = yb[...] * in_low
    fq[12:20, :, 384:512] = yb[...] * in_high
    fq[20:22, :, 384:512] = yz[4:6] * in_low[0:2] * keep_high
    known = fq[1:22, :, 0:512].reshape(336, 512)
    px[1:22] = dot(known, cst[0:512, 0:256]).astype(BF16).reshape(21, 16, 256)
    cross_x = [send(px.at[1:22], fq.at[1:22, :, 512:768], s1, r1, 9, (ox, gy, gz))]
    plane_mid = dot(known, cst[512:1024, 0:128])
    cross_x[0].wait_recv()
    plane_mid = plane_mid + dot(fq[1:22, :, 512:768].reshape(336, 256), cst[1024:1280, 0:128])
    rows = plane_mid.reshape(21, 16, 128)
    rows = jnp.concatenate([rows, rows[0:1]], axis=0).reshape(11, 2, 16, 128)
    odd, even = rows[:, 0], rows[:, 1]
    q_mid = (
        even[1:9]
        + (9.0 / 16.0) * (odd[1:9] + odd[2:10])
        + (-1.0 / 16.0) * (odd[0:8] + odd[3:11])
    ).astype(BF16)
    fm[6:14, :, 0:128] = q_mid
    tops = dot(q_mid.reshape(128, 128), cst[512:640, 256:768]).reshape(8, 16, 512)
    member = lax.broadcasted_iota(jnp.int32, (16, 512), 0)
    group = lax.broadcasted_iota(jnp.int32, (16, 512), 1) // 32
    tops = jnp.sum(jnp.where((member == group)[None], tops, 0.0), axis=1)
    sent, error = [], jnp.zeros((1, 512), F32)
    for z in range(8):
        value = tops[z : z + 1] + error
        sent.append(value.astype(BF16).astype(F32))
        error = value - sent[-1]
    sent = jnp.concatenate(sent, axis=0)
    gath[gz] = jnp.concatenate([sent[:, 0:256], sent[:, 256:512]], axis=0).astype(BF16)

    def gather(d, slot):
        return pltpu.make_async_remote_copy(
            src_ref=gath.at[slot], dst_ref=gath.at[slot], send_sem=sg.at[d], recv_sem=rg.at[slot],
            device_id=(gx, gy, lax.rem(gz + d, nz)), device_id_type=MESH,
        )

    @pl.loop(1, nz)
    def _(d):
        gather(d, gz).start()

    ways = [
        (fm.at[8:14, :, 0:128], fm.at[0:6, :, 128:256], (gx, oy, up)),
        (fm.at[6:12, :, 0:128], fm.at[14:20, :, 128:256], (gx, oy, down)),
        (fm.at[8:14, :, 0:128], fm.at[0:6, :, 0:128], (gx, gy, up)),
        (fm.at[6:12, :, 0:128], fm.at[14:20, :, 0:128], (gx, gy, down)),
        (fm.at[6:14, :, 0:128], fm.at[6:14, :, 128:256], (gx, oy, gz)),
    ]
    two = [send(src, dst, s2, r2, i, peer) for i, (src, dst, peer) in enumerate(ways)]

    for copy in one[5:]:
        copy.wait_recv()
    for where, other, keep in (
        (slice(0, 1), yz[0:1] * in_high[0:1], keep_low), (slice(22, 24), yz[6:8] * in_low[0:2], keep_high)
    ):
        count = where.stop - where.start
        fq[where, :, 0:384] = fq[where, :, 0:384] * keep
        fq[where, :, 384:512] = other * keep
        px[where] = dot(fq[where, :, 0:512].reshape(16 * count, 512), cst[0:512, 0:256]).astype(
            BF16
        ).reshape(count, 16, 256)
    cross_x += [
        send(px.at[0:1], fq.at[0:1, :, 512:768], s1, r1, 10, (ox, gy, gz)),
        send(px.at[22:24], fq.at[22:24, :, 512:768], s1, r1, 11, (ox, gy, gz)),
    ]
    for copy in cross_x[1:]:
        copy.wait_recv()
    fpad[...] = dot(fq[...].reshape(384, 768), cst[1280:2048, :]).astype(BF16)
    for g in range(2):
        total = None
        for c in range(9):
            term = dot_t(tfine[c], fpad[16 * c : 16 * c + 256, 256 * g : 256 * g + 512])
            total = term if total is None else total + term
        sfine[g] = total

    for d in far_first:
        gather(d, lax.rem(gz + nz - d, nz)).wait_recv()

    got = gath[...].reshape(512, 256)
    fields = jnp.concatenate([dot(ezr[h, 0], got) + dot(ezr[h, 1], got) for h in range(2)], axis=1)
    lane = lax.broadcasted_iota(jnp.int32, (16, 128), 1) // 32
    for j in range(4):
        tile = fields[:, 128 * j : 128 * j + 128]
        turns = [tile] + [pltpu.roll(tile, 32 * t, 1) for t in range(1, 4)]
        for i in range(4):
            m = 4 * j + i
            for t in range(2):
                block = None
                for s in range(4):
                    g = 4 * t + s
                    piece = turns[(s - i) % 4][16 * g : 16 * g + 16]
                    block = piece if block is None else jnp.where(lane == s, piece, block)
                amat[16 * m : 16 * m + 16, 128 * t : 128 * t + 128] = block
    high, low = split(amat[...])
    share = dot(high[0:128], wlo[0]) + dot(high[128:256], whi[0])
    share = share + (dot(low[0:128], wlo[0]) + dot(low[128:256], whi[0]))
    share = share + (dot(high[0:128], wlo[1]) + dot(high[128:256], whi[1]))
    share = jnp.swapaxes(share.reshape(8, 16, 512), 0, 1)
    for w in range(4):
        dmat[w] = share[0:10, :, 128 * w : 128 * w + 128]
    ways = [(oy + 2 * gx, (gx, oy, gz)), (oy + 2 * ox, (ox, oy, gz)), (gy + 2 * ox, (ox, gy, gz))]
    three = [send(dmat.at[w], rmat.at[i], s3, r3, i, peer) for i, (w, peer) in enumerate(ways)]

    for copy in two:
        copy.wait_recv()
    fm[0:6, :, 0:256] = fm[0:6, :, 0:256] * keep_low
    fm[14:20, :, 0:256] = fm[14:20, :, 0:256] * keep_high
    cross_m = send(fm.at[:, :, 0:256], fm.at[:, :, 256:512], s2, r2, 5, (ox, gy, gz))

    cross_m.wait_recv()
    mpad[...] = dot(fm[...].reshape(320, 512), cst[2048:2560, :]).astype(BF16)
    for g in range(2):
        total = None
        for c in range(9):
            term = dot_t(mpad[16 * c : 16 * c + 192, 256 * g : 256 * g + 512], tmid[c])
            total = term if total is None else total + term
        smid[:, 256 * g : 256 * g + 256] = total

    def trimmed(mid):
        spot = lax.broadcasted_iota(jnp.int32, mid.shape, 0) - 2 + 8 * gz
        return jnp.where((spot >= 0) & (spot < 8 * nz), mid, 0.0)

    mid = trimmed(smid[...].reshape(12, 16, 512))
    fine = interleave(mid[2:10], widen(mid[1:12], 8)).reshape(256, 512)
    high, low = split(fine)
    back = cst[768:1152, 256:768]
    total = dot_t(back, high) + dot_t(back, low)
    total = total + sfine[...].reshape(16, 32, 256)[:, 0:24].reshape(384, 256)
    sfine_own = total

    for copy in one + cross_x + two:
        copy.wait_send()

    @pl.loop(1, nz)
    def _(d):
        gather(d, gz).wait_send()

    for copy in three:
        copy.wait_recv()
    top = (dmat[variant] + rmat[2]) + (rmat[0] + rmat[1])
    mid = interleave(top[2:8], widen(top[1:10], 6))
    mid = trimmed(mid)
    fine = interleave(mid[2:10], widen(mid[1:12], 8))
    lower = lax.broadcasted_iota(jnp.int32, (16, 8, 128), 2) < 64
    fine = jnp.concatenate(
        [jnp.where(lower, fine, 0.0), jnp.where(lower, 0.0, fine)], axis=1
    ).reshape(256, 128)
    high, low = split(fine)
    up_high, up_low = cst[0:384, 384:512], cst[0:384, 512:640]
    result = dot_t(up_high, high) + (dot_t(up_high, low) + dot_t(up_low, high)) + sfine_own
    out_ref[...] = result.reshape(16, 24, 256)

    for copy in [cross_m] + three:
        copy.wait_send()


def solution(mesh):
    whole, spread = constants()
    nz = mesh.shape["gz"]
    vmem = pl.BlockSpec(memory_space=pltpu.VMEM)
    dma = pltpu.SemaphoreType.DMA

    def per_device(charges, kernel_fine, kernel_mid, gauss_width, gauss_weight):
        return pl.pallas_call(
            kernel,
            out_shape=jax.ShapeDtypeStruct((16, 24, 256), F32),
            in_specs=[pl.BlockSpec(memory_space=pltpu.HBM)] * 7,
            out_specs=vmem,
            scratch_shapes=[
                pltpu.VMEM((16, 24, 256), BF16),
                pltpu.VMEM((9, 9, 9), BF16),
                pltpu.VMEM((9, 9, 9), BF16),
                pltpu.SMEM((GAUSS,), F32),
                pltpu.SMEM((GAUSS,), F32),
                pltpu.VMEM((32, 512), F32),
                pltpu.VMEM((16, 512), F32),
                pltpu.VMEM((ROWS_C, 768), BF16),
                pltpu.VMEM((24, 16, 768), BF16),
                pltpu.VMEM((8, 16, 128), BF16),
                pltpu.VMEM((8, 16, 128), BF16),
                pltpu.VMEM((8, 16, 128), BF16),
                pltpu.VMEM((24, 16, 256), BF16),
                pltpu.VMEM((384, 768), BF16),
                pltpu.VMEM((9, 256, 512), BF16),
                pltpu.VMEM((9, 256, 512), BF16),
                pltpu.VMEM((20, 16, 512), BF16),
                pltpu.VMEM((320, 768), BF16),
                pltpu.VMEM((nz, 16, 256), BF16),
                pltpu.VMEM((2, 256, 256), F32),
                pltpu.VMEM((192, 512), F32),
                pltpu.VMEM((256, 256), F32),
                pltpu.VMEM((4, 10, 8, 128), F32),
                pltpu.VMEM((3, 10, 8, 128), F32),
                pltpu.VMEM((2, 2, 128, 512), BF16),
                pltpu.VMEM((2, 256, 512), BF16),
                pltpu.VMEM((2, 256, 512), BF16),
                dma((8,)),
                dma((12,)), dma((12,)),
                dma((6,)), dma((6,)),
                dma((nz,)), dma((nz,)),
                dma((3,)), dma((3,)),
            ],
            compiler_params=pltpu.CompilerParams(
                collective_id=0, has_side_effects=True, vmem_limit_bytes=40 * 2**20
            ),
        )(
            *[
                pltpu.with_memory_space_constraint(a, pltpu.HBM)
                for a in (
                    charges, kernel_fine, kernel_mid, gauss_width, gauss_weight,
                    jnp.asarray(whole), jnp.asarray(spread),
                )
            ]
        )

    placed = (P("gx", "gy", "gz"), P(), P(), P(), P())
    return jax.shard_map(
        per_device, mesh=mesh, in_specs=placed, out_specs=P("gx", "gy", "gz"), check_vma=False
    )
```

```python
import jax
import jax.numpy as jnp
import numpy as np
import ml_dtypes
from jax import lax
from jax.experimental import pallas as pl
from jax.experimental.pallas import tpu as pltpu
from jax.sharding import PartitionSpec as P

M = 16
GAUSS = 8
MESH = pl.DeviceIdType.MESH
F32 = jnp.float32
BF16 = jnp.bfloat16


def weight(offset):
    return {0: 1.0, 1: 9 / 16, 3: -1 / 16}.get(abs(offset), 0.0)


def halo_list(side, size):
    if side == 0:
        return [size, size + 1, size + 2, size + 3, size + 5, None, None, None]
    return [-9, -7, -6, -5, -4, -3, -2, -1]


def extra_list(side, size):
    return [size + 1] if side == 0 else [-3, -1]


def cross(xs, ys):
    return [None if (x is None or y is None) else (x, y) for x in xs for y in ys]


def moved(coords, dx, dy):
    return [None if c is None else (c[0] + dx, c[1] + dy) for c in coords]


def padded(coords, size):
    return coords + [None] * (size - len(coords))


def picker(source, target):
    table = np.zeros((len(source), len(target)), np.float32)
    for j, c in enumerate(target):
        for i, other in enumerate(source):
            if c is not None and c == other:
                table[i, j] = 1.0
    return table


def weights_between(fine, coarse):
    table = np.zeros((len(fine), len(coarse)), np.float32)
    for i, f in enumerate(fine):
        if f is None:
            continue
        for j, c in enumerate(coarse):
            if c is not None:
                table[i, j] = weight(f[0] - 2 * c[0]) * weight(f[1] - 2 * c[1])
    return table


ROWS_A = 512
ROWS_C = 2560


def plane(gx, gy):
    yl = [24, 25, 26, 27] if gy == 0 else [-4, -3, -2, -1]
    xl = halo_list(gx, 16)
    own = cross(range(16), range(24))
    edge = cross(range(16), yl)
    fine = own + edge + edge + cross(xl, list(range(24)) + yl + [None] * 4)
    mid_own = cross(range(8), range(12))
    mid = padded(mid_own + cross(extra_list(gx, 8), range(12)), 128)
    return own, fine, mid_own, mid


def constants():
    whole = np.zeros((4, ROWS_C, 768), np.float32)
    spread = np.full((4, 32, 512), 1e30, np.float32)
    for gx in range(2):
        for gy in range(2):
            v = gx * 2 + gy
            own, fine, mid_own, mid = plane(gx, gy)
            out = whole[v]
            dy = 24 if gy == 0 else -24
            dx = 16 if gx == 0 else -16
            other_y = plane(gx, 1 - gy)[1]
            other_x = plane(1 - gx, gy)[1]
            out[0:384, 256:384] = picker(own, moved(other_y[384:512], 0, dy))
            out[0:512, 0:256] = picker(fine[:512], moved(other_x[512:768], dx, 0))
            xs = range(0, 7) if gx == 0 else range(-3, 4)
            ys = range(0, 9) if gy == 0 else range(-3, 6)
            window = padded(cross(xs, ys), 64)
            inside = cross(
                range(0, 10) if gx == 0 else range(-2, 8), range(0, 14) if gy == 0 else range(-2, 12)
            )
            up = weights_between(own, inside).astype(np.float64) @ weights_between(inside, window)
            up = np.concatenate([up, up], axis=1)
            high = up.astype(ml_dtypes.bfloat16).astype(np.float64)
            out[0:384, 384:512] = high
            out[0:384, 512:640] = up - high
            rz = np.zeros((256, 128), np.float32)
            for j in range(256):
                for i in range(128):
                    rz[j, i] = weight(j - 2 * i)
            empty = np.zeros((32, 8, 128), np.float32)
            rz = rz.reshape(32, 8, 128)
            out[0:512, 640:768] = np.stack([rz, empty], axis=1).reshape(512, 128)
            out[512:1024, 128:256] = np.stack([empty, rz], axis=1).reshape(512, 128)
            out[512:1280, 0:128] = weights_between(fine, mid)
            top = cross(range(4), list(range(8)) if gy == 0 else list(range(-1, 6)) + [None])
            out[512:640, 256:768] = np.tile(weights_between(mid, top), (1, 16))
            lanes = [c if c in set(inside) else None for c in cross(range(-2, 14), range(-2, 30))]
            out[768:1152, 256:768] = weights_between(own, lanes)
            out[1280:2048] = picker(fine, cross(range(-4, 20), range(-4, 28)))
            blocks = []
            for bx in (0, dx // 2):
                for by in (0, dy // 2):
                    blocks += padded(moved(mid_own, bx, by), 128)
            out[2048:2560] = picker(blocks, cross(range(-6, 18), range(-6, 26)))
            for i, c in enumerate(top):
                if c is None:
                    continue
                for wx in range(2):
                    for wy in range(2):
                        for xi in range(7):
                            for yi in range(9):
                                d = (4 * gx + c[0] - wx - xi) ** 2 + (6 * gy + c[1] - 3 * wy - yi) ** 2
                                lane = (wx * 2 + wy) * 128 + xi * 9 + yi
                                spread[v, i, lane] = d
                                spread[v, i, lane + 64] = d
    return whole.astype(ml_dtypes.bfloat16), spread


def dot(a, b):
    return lax.dot_general(a, b, (((1,), (0,)), ((), ())), preferred_element_type=F32)


def dot_t(a, b):
    return lax.dot_general(a, b, (((1,), (1,)), ((), ())), preferred_element_type=F32)


def split(a):
    high = a.astype(BF16)
    return high, (a - high.astype(F32)).astype(BF16)


def widen(a, count):
    near, far = 9.0 / 16.0, -1.0 / 16.0
    odd = near * (a[1 : count + 1] + a[2 : count + 2]) + far * (a[0:count] + a[3 : count + 3])
    return odd


def interleave(even, odd):
    both = jnp.concatenate([even[:, None], odd[:, None]], axis=1)
    return both.reshape((2 * even.shape[0],) + even.shape[1:])


def kernel(
    q_hbm, kf_hbm, km_hbm, gw_hbm, gg_hbm, cst_hbm, spread_hbm, out_ref,
    q_ref, kf_ref, km_ref, gw_ref, gg_ref, spread_ref, base, cst, fq, py, yb, yz, px, fpad, tfine, tmid, fm, mpad, gath, sfine, smid, amat, dmat, rmat, ezr, wlo, whi,
    cst_sem, s1, r1, s2, r2, sg, rg, s3, r3,
):
    gx, gy, gz = lax.axis_index("gx"), lax.axis_index("gy"), lax.axis_index("gz")
    nz = lax.axis_size("gz")
    ox, oy = 1 - gx, 1 - gy
    up, down = lax.rem(gz + 1, nz), lax.rem(gz + nz - 1, nz)
    variant = gx * 2 + gy

    first = pltpu.make_async_copy(
        cst_hbm.at[variant, pl.ds(0, ROWS_A)], cst.at[pl.ds(0, ROWS_A)], cst_sem.at[0]
    )
    rest = pltpu.make_async_copy(
        cst_hbm.at[variant, pl.ds(ROWS_A, ROWS_C - ROWS_A)],
        cst.at[pl.ds(ROWS_A, ROWS_C - ROWS_A)],
        cst_sem.at[1],
    )
    inputs = [
        pltpu.make_async_copy(src, dst, cst_sem.at[2 + i])
        for i, (src, dst) in enumerate(
            (
                (q_hbm, q_ref), (kf_hbm, kf_ref), (km_hbm, km_ref), (gw_hbm, gw_ref),
                (gg_hbm, gg_ref), (spread_hbm.at[variant], spread_ref),
            )
        )
    ]
    for copy in inputs[:2]:
        copy.start()
    first.start()
    for copy in inputs[2:]:
        copy.start()
    rest.start()

    far_first = sorted(
        range(1, nz), key=lambda d: -min(d // 8, 4 - d // 8) - min(d // 2 % 4, 4 - d // 2 % 4)
    )
    barrier = pltpu.get_barrier_semaphore()
    for peer in ((ox, gy, gz), (gx, oy, gz), (ox, oy, gz), (gx, oy, up), (gx, oy, down)):
        pl.semaphore_signal(barrier, inc=1, device_id=peer, device_id_type=MESH)

    for d in far_first:
        pl.semaphore_signal(
            barrier, inc=1, device_id=(gx, gy, lax.rem(gz + d, nz)), device_id_type=MESH
        )

    inputs[0].wait()
    turned = q_ref[...].astype(F32).reshape(384, 256).T.astype(BF16)
    fq[4:20, :, 0:384] = turned.reshape(16, 16, 384)
    first.wait()
    edge = dot(turned, cst[0:384, 256:384]).reshape(16, 16, 128)
    low_half = lax.broadcasted_iota(jnp.int32, (8, 16, 128), 2) < 64
    py[...] = jnp.where(low_half, edge[0:8], edge[8:16]).astype(BF16)

    def build(k_ref, table):
        lane = lax.broadcasted_iota(jnp.int32, (9, 512), 1)
        row = lax.broadcasted_iota(jnp.int32, (9, 512), 0)
        total = jnp.zeros((9, 512), F32)
        for a in range(9):
            place = (lane == row + 32 * a).astype(F32).astype(BF16)
            total = total + lax.dot_general(
                k_ref[a], place, (((0,), (0,)), ((), ())), preferred_element_type=F32
            )
        base[0:9] = total

        @pl.loop(0, 9)
        def _(c):
            line = jnp.broadcast_to(base[pl.ds(c, 1)], (16, 512))
            strip = pltpu.roll(line, 0, 1, stride=1, stride_axis=0)
            for i in range(8):
                part = pltpu.roll(strip, 16 * i, 1).astype(BF16)
                table[c, 16 * i : 16 * i + 16, :] = part
                table[c, 128 + 16 * i : 144 + 16 * i, 0:128] = part[:, 384:512]
                table[c, 128 + 16 * i : 144 + 16 * i, 128:512] = part[:, 0:384]

    pl.semaphore_wait(barrier, nz - 1 + 5)

    def send(src, dst, sems, recvs, i, peer):
        copy = pltpu.make_async_remote_copy(
            src_ref=src, dst_ref=dst, send_sem=sems.at[i], recv_sem=recvs.at[i],
            device_id=peer, device_id_type=MESH,
        )
        copy.start()
        return copy

    ways = [
        (py.at[5:8], yz.at[1:4], (gx, oy, up)),
        (py.at[0:2], yz.at[4:6], (gx, oy, down)),
        (fq.at[17:20, :, 0:384], fq.at[1:4, :, 0:384], (gx, gy, up)),
        (fq.at[4:6, :, 0:384], fq.at[20:22, :, 0:384], (gx, gy, down)),
        (py, yb, (gx, oy, gz)),
        (py.at[4:5], yz.at[0:1], (gx, oy, up)),
        (py.at[2:4], yz.at[6:8], (gx, oy, down)),
        (fq.at[16:17, :, 0:384], fq.at[0:1, :, 0:384], (gx, gy, up)),
        (fq.at[6:8, :, 0:384], fq.at[22:24, :, 0:384], (gx, gy, down)),
    ]
    one = [send(src, dst, s1, r1, i, peer) for i, (src, dst, peer) in enumerate(ways)]

    for copy in inputs[1:]:
        copy.wait()
    build(kf_ref, tfine)
    build(km_ref, tmid)
    rest.wait()
    node = gz * 4 - 3 + lax.broadcasted_iota(jnp.int32, (16, 128), 0)
    gap = (node - lax.broadcasted_iota(jnp.int32, (16, 128), 1)).astype(F32)
    exists = (node >= 0) & (node < 4 * nz)
    half = lax.rem(lax.broadcasted_iota(jnp.int32, (32, 512), 1), 128) < 64
    parts = []
    for g in range(GAUSS):
        width = jnp.full((16, 128), gw_ref[g], F32)
        ratio = gap / width
        parts.append(jnp.where(exists, jnp.exp(-(ratio * ratio)) / jnp.sqrt(width), 0.0))
        width = jnp.full((32, 512), gw_ref[g], F32)
        both = jnp.exp(-(spread_ref[...] / (width * width))) * (gg_ref[g] / width)
        for table, keep in ((wlo, half), (whi, jnp.logical_not(half))):
            high, low = split(jnp.where(keep, both, 0.0))
            table[0, 32 * g : 32 * g + 32] = high
            table[1, 32 * g : 32 * g + 32] = low
    ez = jnp.concatenate(parts, axis=0)
    high, low = split(ez)
    low2 = (ez - high.astype(F32) - low.astype(F32)).astype(BF16)
    for h, rz in enumerate((cst[0:512, 640:768], cst[512:1024, 128:256])):
        first_half, second = split(dot_t(high, rz) + dot_t(low, rz) + dot_t(low2, rz))
        ezr[h, 0] = first_half
        ezr[h, 1] = second

    for copy in one[:5]:
        copy.wait_recv()
    keep_low = (gz > 0).astype(F32).astype(BF16)
    keep_high = (gz < nz - 1).astype(F32).astype(BF16)
    in_low = low_half.astype(F32).astype(BF16)
    in_high = jnp.logical_not(low_half).astype(F32).astype(BF16)
    fq[1:4, :, 0:384] = fq[1:4, :, 0:384] * keep_low
    fq[20:22, :, 0:384] = fq[20:22, :, 0:384] * keep_high
    fq[1:4, :, 384:512] = yz[1:4] * in_high[0:3] * keep_low
    fq[4:12, :, 384:512] = yb[...] * in_low
    fq[12:20, :, 384:512] = yb[...] * in_high
    fq[20:22, :, 384:512] = yz[4:6] * in_low[0:2] * keep_high
    known = fq[1:22, :, 0:512].reshape(336, 512)
    px[1:22] = dot(known, cst[0:512, 0:256]).astype(BF16).reshape(21, 16, 256)
    cross_x = [send(px.at[1:22], fq.at[1:22, :, 512:768], s1, r1, 9, (ox, gy, gz))]
    plane_mid = dot(known, cst[512:1024, 0:128])
    cross_x[0].wait_recv()
    plane_mid = plane_mid + dot(fq[1:22, :, 512:768].reshape(336, 256), cst[1024:1280, 0:128])
    rows = plane_mid.reshape(21, 16, 128)
    rows = jnp.concatenate([rows, rows[0:1]], axis=0).reshape(11, 2, 16, 128)
    odd, even = rows[:, 0], rows[:, 1]
    q_mid = (
        even[1:9]
        + (9.0 / 16.0) * (odd[1:9] + odd[2:10])
        + (-1.0 / 16.0) * (odd[0:8] + odd[3:11])
    ).astype(BF16)
    fm[6:14, :, 0:128] = q_mid
    tops = dot(q_mid.reshape(128, 128), cst[512:640, 256:768]).reshape(8, 16, 512)
    member = lax.broadcasted_iota(jnp.int32, (16, 512), 0)
    group = lax.broadcasted_iota(jnp.int32, (16, 512), 1) // 32
    tops = jnp.sum(jnp.where((member == group)[None], tops, 0.0), axis=1)
    sent, error = [], jnp.zeros((1, 512), F32)
    for z in range(8):
        value = tops[z : z + 1] + error
        sent.append(value.astype(BF16).astype(F32))
        error = value - sent[-1]
    sent = jnp.concatenate(sent, axis=0)
    gath[gz] = jnp.concatenate([sent[:, 0:256], sent[:, 256:512]], axis=0).astype(BF16)

    def gather(d, slot):
        return pltpu.make_async_remote_copy(
            src_ref=gath.at[slot], dst_ref=gath.at[slot], send_sem=sg.at[d], recv_sem=rg.at[slot],
            device_id=(gx, gy, lax.rem(gz + d, nz)), device_id_type=MESH,
        )

    @pl.loop(1, nz)
    def _(d):
        gather(d, gz).start()

    ways = [
        (fm.at[9:14, :, 0:128], fm.at[1:6, :, 128:256], (gx, oy, up)),
        (fm.at[6:12, :, 0:128], fm.at[14:20, :, 128:256], (gx, oy, down)),
        (fm.at[9:14, :, 0:128], fm.at[1:6, :, 0:128], (gx, gy, up)),
        (fm.at[6:12, :, 0:128], fm.at[14:20, :, 0:128], (gx, gy, down)),
        (fm.at[6:14, :, 0:128], fm.at[6:14, :, 128:256], (gx, oy, gz)),
    ]
    two = [send(src, dst, s2, r2, i, peer) for i, (src, dst, peer) in enumerate(ways)]

    for copy in one[5:]:
        copy.wait_recv()
    for where, other, keep in (
        (slice(0, 1), yz[0:1] * in_high[0:1], keep_low), (slice(22, 24), yz[6:8] * in_low[0:2], keep_high)
    ):
        count = where.stop - where.start
        fq[where, :, 0:384] = fq[where, :, 0:384] * keep
        fq[where, :, 384:512] = other * keep
        px[where] = dot(fq[where, :, 0:512].reshape(16 * count, 512), cst[0:512, 0:256]).astype(
            BF16
        ).reshape(count, 16, 256)
    cross_x += [
        send(px.at[0:1], fq.at[0:1, :, 512:768], s1, r1, 10, (ox, gy, gz)),
        send(px.at[22:24], fq.at[22:24, :, 512:768], s1, r1, 11, (ox, gy, gz)),
    ]
    for copy in cross_x[1:]:
        copy.wait_recv()
    fpad[...] = dot(fq[...].reshape(384, 768), cst[1280:2048, :]).astype(BF16)
    for g in range(2):
        total = None
        for c in range(9):
            term = dot_t(tfine[c], fpad[16 * c : 16 * c + 256, 256 * g : 256 * g + 512])
            total = term if total is None else total + term
        sfine[g] = total

    for d in far_first:
        gather(d, lax.rem(gz + nz - d, nz)).wait_recv()

    got = gath[...].reshape(512, 256)
    fields = jnp.concatenate([dot(ezr[h, 0], got) + dot(ezr[h, 1], got) for h in range(2)], axis=1)
    lane = lax.broadcasted_iota(jnp.int32, (16, 128), 1) // 32
    for j in range(4):
        tile = fields[:, 128 * j : 128 * j + 128]
        turns = [tile] + [pltpu.roll(tile, 32 * t, 1) for t in range(1, 4)]
        for i in range(4):
            m = 4 * j + i
            for t in range(2):
                block = None
                for s in range(4):
                    g = 4 * t + s
                    piece = turns[(s - i) % 4][16 * g : 16 * g + 16]
                    block = piece if block is None else jnp.where(lane == s, piece, block)
                amat[16 * m : 16 * m + 16, 128 * t : 128 * t + 128] = block
    high, low = split(amat[...])
    share = dot(high[0:128], wlo[0]) + dot(high[128:256], whi[0])
    share = share + (dot(low[0:128], wlo[0]) + dot(low[128:256], whi[0]))
    share = share + (dot(high[0:128], wlo[1]) + dot(high[128:256], whi[1]))
    share = jnp.swapaxes(share.reshape(8, 16, 512), 0, 1)
    for w in range(4):
        dmat[w] = share[1:10, :, 128 * w : 128 * w + 128]
    ways = [(oy + 2 * gx, (gx, oy, gz)), (oy + 2 * ox, (ox, oy, gz)), (gy + 2 * ox, (ox, gy, gz))]
    three = [send(dmat.at[w], rmat.at[i], s3, r3, i, peer) for i, (w, peer) in enumerate(ways)]

    for copy in two:
        copy.wait_recv()
    fm[0:1, :, 0:256] = jnp.zeros((1, 16, 256), BF16)
    fm[1:6, :, 0:256] = fm[1:6, :, 0:256] * keep_low
    fm[14:20, :, 0:256] = fm[14:20, :, 0:256] * keep_high
    cross_m = send(fm.at[:, :, 0:256], fm.at[:, :, 256:512], s2, r2, 5, (ox, gy, gz))

    cross_m.wait_recv()
    mpad[...] = dot(fm[...].reshape(320, 512), cst[2048:2560, :]).astype(BF16)
    for g in range(2):
        total = None
        for c in range(9):
            term = dot_t(mpad[16 * c : 16 * c + 192, 256 * g : 256 * g + 512], tmid[c])
            total = term if total is None else total + term
        smid[:, 256 * g : 256 * g + 256] = total

    def trimmed(mid):
        spot = lax.broadcasted_iota(jnp.int32, mid.shape, 0) - 2 + 8 * gz
        return jnp.where((spot >= 0) & (spot < 8 * nz), mid, 0.0)

    mid = trimmed(smid[...].reshape(12, 16, 512))
    fine = interleave(mid[2:10], widen(mid[1:12], 8)).reshape(256, 512)
    high, low = split(fine)
    back = cst[768:1152, 256:768]
    total = dot_t(back, high) + dot_t(back, low)
    total = total + sfine[...].reshape(16, 32, 256)[:, 0:24].reshape(384, 256)
    sfine_own = total

    for copy in one + cross_x + two:
        copy.wait_send()

    @pl.loop(1, nz)
    def _(d):
        gather(d, gz).wait_send()

    for copy in three:
        copy.wait_recv()
    top = (dmat[variant] + rmat[2]) + (rmat[0] + rmat[1])
    mid = interleave(top[1:7], widen(top, 6))
    mid = trimmed(mid)
    fine = interleave(mid[2:10], widen(mid[1:12], 8))
    lower = lax.broadcasted_iota(jnp.int32, (16, 8, 128), 2) < 64
    fine = jnp.concatenate(
        [jnp.where(lower, fine, 0.0), jnp.where(lower, 0.0, fine)], axis=1
    ).reshape(256, 128)
    high, low = split(fine)
    up_high, up_low = cst[0:384, 384:512], cst[0:384, 512:640]
    result = dot_t(up_high, high) + (dot_t(up_high, low) + dot_t(up_low, high)) + sfine_own
    out_ref[...] = result.reshape(16, 24, 256)

    for copy in [cross_m] + three:
        copy.wait_send()


def solution(mesh):
    whole, spread = constants()
    nz = mesh.shape["gz"]
    vmem = pl.BlockSpec(memory_space=pltpu.VMEM)
    dma = pltpu.SemaphoreType.DMA

    def per_device(charges, kernel_fine, kernel_mid, gauss_width, gauss_weight):
        return pl.pallas_call(
            kernel,
            out_shape=jax.ShapeDtypeStruct((16, 24, 256), F32),
            in_specs=[pl.BlockSpec(memory_space=pltpu.HBM)] * 7,
            out_specs=vmem,
            scratch_shapes=[
                pltpu.VMEM((16, 24, 256), BF16),
                pltpu.VMEM((9, 9, 9), BF16),
                pltpu.VMEM((9, 9, 9), BF16),
                pltpu.SMEM((GAUSS,), F32),
                pltpu.SMEM((GAUSS,), F32),
                pltpu.VMEM((32, 512), F32),
                pltpu.VMEM((16, 512), F32),
                pltpu.VMEM((ROWS_C, 768), BF16),
                pltpu.VMEM((24, 16, 768), BF16),
                pltpu.VMEM((8, 16, 128), BF16),
                pltpu.VMEM((8, 16, 128), BF16),
                pltpu.VMEM((8, 16, 128), BF16),
                pltpu.VMEM((24, 16, 256), BF16),
                pltpu.VMEM((384, 768), BF16),
                pltpu.VMEM((9, 256, 512), BF16),
                pltpu.VMEM((9, 256, 512), BF16),
                pltpu.VMEM((20, 16, 512), BF16),
                pltpu.VMEM((320, 768), BF16),
                pltpu.VMEM((nz, 16, 256), BF16),
                pltpu.VMEM((2, 256, 256), F32),
                pltpu.VMEM((192, 512), F32),
                pltpu.VMEM((256, 256), F32),
                pltpu.VMEM((4, 9, 8, 128), F32),
                pltpu.VMEM((3, 9, 8, 128), F32),
                pltpu.VMEM((2, 2, 128, 512), BF16),
                pltpu.VMEM((2, 256, 512), BF16),
                pltpu.VMEM((2, 256, 512), BF16),
                dma((8,)),
                dma((12,)), dma((12,)),
                dma((6,)), dma((6,)),
                dma((nz,)), dma((nz,)),
                dma((3,)), dma((3,)),
            ],
            compiler_params=pltpu.CompilerParams(
                collective_id=0, has_side_effects=True, vmem_limit_bytes=40 * 2**20
            ),
        )(
            *[
                pltpu.with_memory_space_constraint(a, pltpu.HBM)
                for a in (
                    charges, kernel_fine, kernel_mid, gauss_width, gauss_weight,
                    jnp.asarray(whole), jnp.asarray(spread),
                )
            ]
        )

    placed = (P("gx", "gy", "gz"), P(), P(), P(), P())
    return jax.shard_map(
        per_device, mesh=mesh, in_specs=placed, out_specs=P("gx", "gy", "gz"), check_vma=False
    )
```
